32 devices in a mesh: ctx: 16 (over z, y, x), kv: 2 (over core).
Axes of the slice: x: 2, y: 2, z: 4, core: 2. Of those that a mesh axis runs over, the one named last changes fastest.
Arguments:
- cache_keys: bfloat16 [8192, 1024], P('ctx', 'kv'), may hold values from -6 to 6
- cache_values: bfloat16 [8192, 1024], P('ctx', 'kv'), may hold values from -6 to 6
- importance: bfloat16 [8, 8192], P('kv', 'ctx'), may hold values from 0.099609375 to 10
- assignment: int32 [8192], P('ctx'), may hold values from 0 to 8191, as said below
- queries: bfloat16 [128, 8192], P(None, 'kv'), may hold values from -40 to 40
Outputs:
- merged_keys: bfloat16 [8192, 1024], P('ctx', 'kv')
- merged_values: bfloat16 [8192, 1024], P('ctx', 'kv')
- attended: bfloat16 [128, 8192], P(None, 'kv')
The draws below stay inside these ranges and needn't reach their ends.
Inputs may be any that keep to these rules, and one draw needn't show every extreme that they name: `assignment`: each entry is the row itself (the row is kept) or a kept row other than itself (the row is evicted and merges into it). The first row of every aligned block of 128 rows is kept and no row merges into it; in every aligned block between a quarter and five twelfths of the rows, rounded down, are evicted. A shard is an aligned block of 512 rows; shard numbers are taken modulo the number of shards. Of the rows of one shard, at most 16 merge into rows of the shard before it and at most 16 into rows of the shard after it, and into rows of every other shard at least 0 and at most 1. The bounds 16 and 1 are reached in every draw.
All inputs are finite; a program needn't handle non-finite values.
Results may differ from the reference program's by a relative error of at most 0.0055.
Values may be sent and summed in bfloat16 or wider, within the bound.
A program may use at most 192 MiB of HBM per device.

```python
import math
import jax
import jax.numpy as jnp
from jax import lax

HQ = 64
KVH = 8
HD = 128
ROWS_DEV = 512
BLOCK = 128
NEAR = 16
FAR = 1
GROUP = 8
QTOT = 128
CTX_ROWS = 8192
N_CTX = 16


def key_field(key):
    normal_part = jax.random.normal(jax.random.fold_in(key, 101), (CTX_ROWS, KVH * HD), jnp.float32)
    return normal_part


def draw_cache_keys(key, part):
    field_values = key_field(key)
    return jnp.clip(field_values, -6.0, 6.0).astype(jnp.bfloat16)


def draw_queries(key, part):
    key = jax.random.fold_in(key, 2)
    drawn = jnp.clip(3.5 * jax.random.normal(key, (QTOT, HQ * HD), jnp.float32), -21.0, 21.0)
    return drawn.astype(jnp.bfloat16)


def draw_assignment(key, part):
    key = jax.random.fold_in(key, 3)
    parts_key = jax.random.split(key, 9)
    block_count = ROWS_DEV // BLOCK
    total_rows = N_CTX * ROWS_DEV
    evicted_count = jax.random.randint(parts_key[0], (N_CTX, block_count, 1), BLOCK // 4, BLOCK * 5 // 12 + 1)
    shuffle = jax.random.randint(parts_key[1], (N_CTX, block_count, BLOCK), 0, 1 << 20) * BLOCK + jnp.arange(BLOCK, dtype=jnp.int32)
    shuffle = shuffle.at[:, :, 0].set(jnp.int32(1 << 30))
    slot_order = jnp.argsort(jnp.argsort(shuffle, axis=2), axis=2)
    evicted = (slot_order < evicted_count).reshape(N_CTX, ROWS_DEV)
    row_ids = jnp.arange(ROWS_DEV, dtype=jnp.int32)
    order_key = jnp.where(evicted, jax.random.randint(parts_key[2], (N_CTX, ROWS_DEV), 0, 1 << 18), 1 << 18) * ROWS_DEV + row_ids
    queue_turn = jnp.argsort(jnp.argsort(order_key, axis=1), axis=1)
    shard_ids = jnp.arange(N_CTX, dtype=jnp.int32)
    far_shards = N_CTX - 3
    back_count = jnp.where(shard_ids == jax.random.randint(parts_key[3], (), 0, N_CTX), NEAR, jax.random.randint(parts_key[4], (N_CTX,), NEAR // 4, NEAR + 1))[:, None]
    ahead_count = jnp.where(shard_ids == jax.random.randint(parts_key[5], (), 0, N_CTX), NEAR, jax.random.randint(parts_key[6], (N_CTX,), NEAR // 4, NEAR + 1))[:, None]
    far_count = jax.random.randint(parts_key[7], (N_CTX,), far_shards * (FAR - 1) + 1, far_shards * FAR + 1)[:, None]
    far_turn = queue_turn - back_count - ahead_count
    step_out = jnp.where(queue_turn < back_count, N_CTX - 1, jnp.where(queue_turn < back_count + ahead_count, 1, jnp.where(far_turn < far_count, 2 + far_turn % far_shards, 0)))
    destination = (shard_ids[:, None] + step_out) % N_CTX
    eligible = jnp.logical_and(jnp.logical_not(evicted), (row_ids % BLOCK != 0)[None, :])
    eligible_int = eligible.astype(jnp.int32)
    running = jnp.cumsum(eligible_int.reshape(total_rows))
    per_shard = jnp.sum(eligible_int, axis=1)
    starts = jnp.cumsum(per_shard) - per_shard
    choose = jax.random.randint(parts_key[8], (N_CTX, ROWS_DEV), 0, 1 << 20) % per_shard[destination]
    wanted = starts[destination] + choose + 1
    target = jnp.searchsorted(running, wanted.reshape(total_rows), side='left').astype(jnp.int32)
    return jnp.where(evicted.reshape(total_rows), target, jnp.arange(total_rows, dtype=jnp.int32))


def block_scale(key, shape, shards, smallest, top_value):
    def one(axis_at, parts):
        draws = jax.random.uniform(jax.random.fold_in(jax.random.fold_in(key, 6), axis_at), (parts,), jnp.float32, smallest / len(shards), top_value / len(shards))
        return jnp.repeat(jnp.exp(draws), shape[axis_at] // parts).reshape((-1,) + (1,) * (len(shape) - axis_at - 1))

    factor_of = one(*shards[0])
    for cut in shards[1:]:
        factor_of = factor_of * one(*cut)
    return factor_of


def normal_values(stream_key, extent, width, bound, cuts=(), kind=jnp.bfloat16):
    entries = width * jax.random.normal(stream_key, extent, jnp.float32)
    if cuts:
        entries = entries * block_scale(stream_key, extent, cuts, -0.22, 0.18)
    return jnp.clip(entries, -bound, bound).astype(kind)


def setup_inputs(seed: int = 0) -> dict:
    key_of = jax.random.split(jax.random.key(seed), 6)
    cache_keys = draw_cache_keys(jax.random.fold_in(key_of[5], 71), 0)
    cache_values = normal_values(key_of[1], (CTX_ROWS, KVH * HD), 1.0, 6.0, ((0, 16), (1, 2)))
    importance = jnp.clip(jnp.exp(math.log(10.0) - 4.609084 * jax.random.uniform(key_of[2], (KVH, CTX_ROWS), jnp.float32) ** block_scale(key_of[2], (KVH, CTX_ROWS), ((0, 2), (1, 16)), -0.2, 0.2)), 0.099609375, 10.0).astype(jnp.bfloat16)
    assignment = draw_assignment(jax.random.fold_in(key_of[5], 71), 0)
    queries = draw_queries(jax.random.fold_in(key_of[5], 71), 0)
    return {"cache_keys": cache_keys, "cache_values": cache_values, "importance": importance, "assignment": assignment, "queries": queries}


def merge_field(source_field, row_weight, assignment, kept_rows, denominator):
    widened = source_field.astype(jnp.float32)
    weighted = widened * row_weight.astype(jnp.float32)[:, None]
    numerator = jnp.zeros(source_field.shape, jnp.float32).at[assignment].add(weighted)
    safe_total = jnp.where(kept_rows, denominator, jnp.float32(1.0))
    blended = jnp.where(kept_rows[:, None], numerator / safe_total[:, None], widened)
    return blended.astype(jnp.bfloat16)


def attend_head(query_block, key_rows, value_rows, kept_rows):
    block_count = CTX_ROWS // ROWS_DEV
    key_blocks = key_rows.reshape(block_count, ROWS_DEV, HD)
    value_blocks = value_rows.reshape(block_count, ROWS_DEV, HD)
    live_blocks = kept_rows.reshape(block_count, ROWS_DEV)
    query_rows = query_block.shape[0]

    def advance(running, pieces):
        peak_score, weight_sum, accumulated = running
        key_piece, value_piece, live_piece = pieces
        scores = jnp.dot(query_block, key_piece.astype(jnp.float32).T) * (HD ** -0.5)
        scores = jnp.where(live_piece[None, :], scores, -jnp.inf)
        new_peak = jnp.maximum(peak_score, jnp.max(scores, axis=1))
        weights = jnp.exp(scores - new_peak[:, None])
        rescale = jnp.exp(peak_score - new_peak)
        rounded = lax.optimization_barrier(weights.astype(jnp.bfloat16)).astype(jnp.float32)
        weight_sum = weight_sum * rescale + jnp.sum(weights, axis=1)
        accumulated = accumulated * rescale[:, None] + jnp.dot(rounded, value_piece.astype(jnp.float32))
        return (new_peak, weight_sum, accumulated), None

    start_state = (jnp.full((query_rows,), -jnp.inf, jnp.float32), jnp.zeros((query_rows,), jnp.float32), jnp.zeros((query_rows, HD), jnp.float32))
    final_state, unused_out = lax.scan(advance, start_state, (key_blocks, value_blocks, live_blocks))
    return final_state[2] / final_state[1][:, None]


def reference(cache_keys, cache_values, importance, assignment, queries):
    row_weight = jnp.sum(importance.astype(jnp.float32), axis=0).astype(jnp.bfloat16)
    kept_rows = assignment == jnp.arange(CTX_ROWS, dtype=jnp.int32)
    denominator = jnp.zeros((CTX_ROWS,), jnp.float32).at[assignment].add(row_weight.astype(jnp.float32))
    grouped = queries.astype(jnp.float32).reshape(QTOT, KVH, GROUP, HD)
    key_parts = []
    value_parts = []
    output_parts = []
    for head_index in range(KVH):
        low = head_index * HD
        merged_key = merge_field(cache_keys[:, low:low + HD], row_weight, assignment, kept_rows, denominator)
        merged_value = merge_field(cache_values[:, low:low + HD], row_weight, assignment, kept_rows, denominator)
        key_parts.append(merged_key)
        value_parts.append(merged_value)
        query_block = grouped[:, head_index].reshape(QTOT * GROUP, HD)
        head_output = attend_head(query_block, merged_key, merged_value, kept_rows)
        output_parts.append(head_output.reshape(QTOT, GROUP * HD))
    merged_keys = jnp.concatenate(key_parts, axis=1)
    merged_values = jnp.concatenate(value_parts, axis=1)
    attended = jnp.concatenate(output_parts, axis=1).astype(jnp.bfloat16)
    return (merged_keys, merged_values, attended)
```

```python
import functools
import math

import jax
import jax.numpy as jnp
from jax import lax
from jax.experimental import pallas as pl
from jax.experimental.pallas import tpu as pltpu
from jax.sharding import PartitionSpec as P

NEAR = 16
LANES = 128
PLANE = 4
MESH = pl.DeviceIdType.MESH
F32 = jnp.float32
BF16 = jnp.bfloat16


def dot(a, b):
    return jnp.dot(a, b, preferred_element_type=F32)


def dot_t(a, b):
    return lax.dot_general(a, b, (((0,), (0,)), ((), ())), preferred_element_type=F32)


def flip(index, step):
    if step == 1:
        return index + 1 - 2 * lax.rem(index, 2)
    if step == 2:
        return index + 2 - 4 * lax.div(index, 2)
    return 3 - index


def combine(parts, coef):
    peak = functools.reduce(jnp.maximum, [m for _, m, _ in parts])
    total, weight = None, None
    for o, m, l in parts:
        factor = jnp.exp2((m - peak) * coef)
        o, l = o * factor, l * factor
        total = o if total is None else total + o
        weight = l if weight is None else weight + l
    return total, peak, weight


def stats(m, l):
    rows = lax.broadcasted_iota(jnp.int32, (8, m.shape[1]), 0)
    shape = (8, m.shape[1])
    return jnp.where(rows == 0, jnp.broadcast_to(m, shape), jnp.broadcast_to(l, shape))


def kernel(
    shards, kv_size, subs, piece,
    k_ref, v_ref, imp_ref, asg_ref, q_ref,
    mk_ref, mv_ref, out_ref,
    kv_send, kv_recv, near_send, near_recv, far_send, far_recv, far_wide, arrived,
    num, q_t, k_ext, v_t,
    l1_send, l1_recv, s1_send, s1_recv, own_o, own_s,
    l2_send, l2_recv, s2_send, s2_recv,
    kv_ss, kv_rs, near_ss, near_rs, far_ss, far_rs,
    l1_ss, l1_rs, s1_ss, s1_rs, l2_ss, l2_rs, s2_ss, s2_rs,
    g2_ss, g2_rs, g1_ss, g1_rs,
):
    me = lax.axis_index("ctx")
    kv = lax.axis_index("kv")
    lo, hi = lax.rem(me, PLANE), lax.div(me, PLANE)
    high = shards // PLANE
    scatter = subs == high
    rows, width = k_ref.shape
    heads = width // LANES
    lanes = q_ref.shape[1]
    group_lanes = lanes // heads
    chunk = lanes // PLANE
    slots = 2 * NEAR + shards
    tiles = 2 * heads
    coef = math.log2(math.e) / math.sqrt(LANES)
    sent = []

    def put(src, dst, ss, rs, target):
        copy = pltpu.make_async_remote_copy(
            src_ref=src, dst_ref=dst, send_sem=ss, recv_sem=rs,
            device_id=target, device_id_type=MESH,
        )
        copy.start()
        sent.append(copy)
        return copy

    barrier = pltpu.get_barrier_semaphore()

    def greet(s, carry):
        pl.semaphore_signal(
            barrier, inc=1, device_id=(lax.rem(me + s, shards), kv), device_id_type=MESH
        )
        return carry

    for s in range(1, kv_size):
        pl.semaphore_signal(
            barrier, inc=1, device_id=(me, lax.rem(kv + s, kv_size)), device_id_type=MESH
        )
    lax.fori_loop(1, shards, greet, 0)

    part_weight = jnp.sum(imp_ref[...].astype(F32), axis=0, keepdims=True)
    kv_send[...] = jnp.broadcast_to(part_weight, (8, rows))
    for s in (0, 1, shards - 1):
        far_recv[s] = jnp.zeros((16, LANES), BF16)
    far_wide[...] = jnp.zeros_like(far_wide)

    pl.semaphore_wait(barrier, shards - 1 + kv_size - 1)
    kv_copies = [
        put(kv_send, kv_recv.at[s], kv_ss.at[s], kv_rs.at[s], (me, lax.rem(kv + s, kv_size)))
        for s in range(1, kv_size)
    ]

    asg = asg_ref[...]
    owner = jnp.right_shift(asg, rows.bit_length() - 1)
    target = jnp.bitwise_and(asg, rows - 1)
    distance = jnp.bitwise_and(owner - me, shards - 1)
    rank_row = lax.broadcasted_iota(jnp.int32, (16, rows), 0)
    distance_16 = jnp.broadcast_to(distance, (16, rows))
    wanted = jnp.where(rank_row == 0, 1, jnp.where(rank_row == 1, shards - 1, -1))
    marks = jnp.where(distance_16 == wanted, 1.0, 0.0).astype(BF16)
    earlier = jnp.where(
        lax.broadcasted_iota(jnp.int32, (rows, rows), 0)
        < lax.broadcasted_iota(jnp.int32, (rows, rows), 1),
        1.0, 0.0,
    ).astype(BF16)
    rank = dot(marks, earlier).astype(jnp.int32)
    key_next = jnp.where(distance == 1, rank[0:1], -1)
    key_prev = jnp.where(distance == shards - 1, rank[1:2], -1)
    far = jnp.where(distance >= 2, jnp.where(distance <= shards - 2, distance, -1), -1)

    def select(key, count):
        index = lax.broadcasted_iota(jnp.int32, (count, rows), 0)
        return jnp.where(jnp.broadcast_to(key, (count, rows)) == index, 1.0, 0.0)

    chosen = jnp.concatenate(
        [select(key_next, NEAR), select(key_prev, NEAR), select(far, shards)], axis=0
    )
    chosen_b = chosen.astype(BF16)
    out_rows = [dot(chosen_b, k_ref[...]), dot(chosen_b, v_ref[...])]
    meta_high = jnp.sum(
        chosen * jnp.right_shift(target, 7).astype(F32), axis=1, keepdims=True
    )
    meta_low = jnp.sum(
        chosen * jnp.bitwise_and(target, LANES - 1).astype(F32), axis=1, keepdims=True
    )
    for d in range(2):
        for part in range(2):
            near_send[d, :, part * width:(part + 1) * width] = out_rows[part][
                d * NEAR:(d + 1) * NEAR
            ].astype(BF16)
    for c in range(tiles):
        part, at = divmod(c, heads)
        far_wide[:, c, :] = out_rows[part][2 * NEAR:, at * LANES:(at + 1) * LANES]

    total_weight = part_weight
    for s, copy in enumerate(kv_copies, 1):
        copy.wait_recv()
        total_weight = total_weight + kv_recv[s, 0:1, :]
    weight = total_weight.astype(BF16).astype(F32)
    meta_weight = jnp.sum(chosen * weight, axis=1, keepdims=True)
    for m, meta in enumerate((meta_weight, meta_high, meta_low)):
        spread = jnp.broadcast_to(meta, (slots, LANES))
        for d in range(2):
            near_send[d, :, 2 * width + m * LANES:2 * width + (m + 1) * LANES] = spread[
                d * NEAR:(d + 1) * NEAR
            ].astype(BF16)
        far_wide[:, tiles + m, :] = spread[2 * NEAR:]
    far_send[...] = far_wide[...].astype(BF16)

    near_copies = [
        put(near_send.at[d], near_recv.at[d], near_ss.at[d], near_rs.at[d],
            (lax.rem(me + step, shards), kv))
        for d, step in enumerate((1, shards - 1))
    ]

    def far_copy(s):
        return pltpu.make_async_remote_copy(
            src_ref=far_send.at[s], dst_ref=far_recv.at[s],
            send_sem=far_ss.at[s], recv_sem=far_rs.at[s],
            device_id=(lax.rem(me + s, shards), kv), device_id_type=MESH,
        )

    def far_start(s, carry):
        far_copy(s).start()
        return carry

    def far_wait(s, carry):
        far_copy(s).wait()
        return carry

    lax.fori_loop(2, shards - 1, far_start, 0)

    home = jnp.where(distance == 0, target, -1)
    home_matrix = jnp.where(
        jnp.broadcast_to(home, (rows, rows))
        == lax.broadcasted_iota(jnp.int32, (rows, rows), 0),
        jnp.broadcast_to(weight, (rows, rows)), 0.0,
    ).astype(BF16)
    num[:, 0:width] = dot(home_matrix, k_ref[...])
    num[:, width:2 * width] = dot(home_matrix, v_ref[...])
    num[:, 2 * width:] = dot(home_matrix, jnp.ones((rows, LANES), BF16))
    for j in range(lanes // LANES):
        at = slice(j * LANES, (j + 1) * LANES)
        q_t[0:LANES, at] = q_ref[:, at].T
    q_t[LANES:, :] = jnp.ones((LANES, lanes), BF16)

    for copy in near_copies:
        copy.wait_recv()
    lax.fori_loop(2, shards - 1, far_wait, 0)

    far_wide[...] = far_recv[...].astype(F32)
    for d in range(2):
        arrived[d * NEAR:(d + 1) * NEAR, 0:2 * width] = near_recv[d, :, 0:2 * width]
    for c in range(tiles):
        arrived[2 * NEAR:, c * LANES:(c + 1) * LANES] = far_wide[:, c, :].astype(BF16)
    arrived[:, 2 * width:] = jnp.ones((slots, LANES), BF16)

    def meta_of(m):
        at = slice(2 * width + m * LANES, 2 * width + (m + 1) * LANES)
        return jnp.concatenate(
            [near_recv[0, :, at].astype(F32), near_recv[1, :, at].astype(F32),
             far_wide[:, tiles + m, :]], axis=0,
        )

    in_weight = meta_of(0)
    in_target = (meta_of(1) * LANES + meta_of(2)).astype(jnp.int32)
    lane = lax.broadcasted_iota(jnp.int32, (slots, LANES), 1)
    spread_t = jnp.concatenate(
        [jnp.where(in_target == lane + b * LANES, in_weight, 0.0) for b in range(rows // LANES)],
        axis=1,
    ).astype(BF16)

    denominator = num[:, 2 * width:] + dot_t(spread_t, arrived[:, 2 * width:])
    kept = denominator > 0.0
    inverse = 1.0 / jnp.where(kept, denominator, 1.0)
    first_lane = lax.broadcasted_iota(jnp.int32, (rows, LANES), 1) == 0
    bias = jnp.where(first_lane, jnp.where(kept, 0.0, -1e30), 0.0).astype(BF16)
    for h in range(heads):
        at = slice(h * LANES, (h + 1) * LANES)
        far_at = slice(width + h * LANES, width + (h + 1) * LANES)
        key = (num[:, at] + dot_t(spread_t, arrived[:, at])) * inverse
        key = jnp.where(kept, key, k_ref[:, at].astype(F32)).astype(BF16)
        mk_ref[:, at] = key
        k_ext[h, :, 0:LANES] = key
        k_ext[h, :, LANES:] = bias
        value = (num[:, far_at] + dot_t(spread_t, arrived[:, far_at])) * inverse
        value = jnp.where(kept, value, v_ref[:, at].astype(F32)).astype(BF16)
        mv_ref[:, at] = value
        v_t[h, 0:LANES, :] = value.T
        v_t[h, LANES:, :] = jnp.ones((16, rows), BF16)

    def attend(column):
        h = lax.div(column, group_lanes)
        queries = q_t[:, pl.ds(pl.multiple_of(column, LANES), piece)]
        score = dot(k_ext[h], queries)
        peak = jnp.max(score, axis=0, keepdims=True)
        prob = jnp.exp2((score - peak) * coef).astype(BF16)
        both = dot(v_t[h], prob)
        return both[0:LANES], peak, both[LANES:LANES + 1]

    def sub_of(u):
        return lax.rem(hi + u, high) if scatter else 0

    order = list(range(1, subs)) + [0]
    l1_copies = {}

    def work(u):
        for s in (3, 1, 2, 0):
            dest = flip(lo, s) if s else lo
            o, m, l = attend(dest * chunk + sub_of(u) * piece)
            if s == 0:
                own_o[u] = o
                own_s[u] = stats(m, l)
                continue
            l1_send[s, u] = o.astype(BF16)
            s1_send[s, u] = stats(m, l)
            to = (hi * PLANE + dest, kv)
            l1_copies[s, u] = (
                put(s1_send.at[s, u], s1_recv.at[s, u], s1_ss.at[s, u], s1_rs.at[s, u], to),
                put(l1_send.at[s, u], l1_recv.at[s, u], l1_ss.at[s, u], l1_rs.at[s, u], to),
            )

    def gather_plane(u):
        parts = [(own_o[u], own_s[u, 0:1, :], own_s[u, 1:2, :])]
        for s in (1, 2, 3):
            for copy in l1_copies[s, u]:
                copy.wait_recv()
            parts.append(
                (l1_recv[s, u].astype(F32), s1_recv[s, u, 0:1, :], s1_recv[s, u, 1:2, :])
            )
        return combine(parts, coef)

    def line(s):
        return (lax.rem(hi + s, high) * PLANE + lo, kv)

    l2_copies = []

    def forward(u):
        o, m, l = gather_plane(u)
        l2_send[u] = o.astype(BF16)
        s2_send[u] = stats(m, l)
        to = line(u)
        l2_copies.append((
            u,
            put(s2_send.at[u], s2_recv.at[u], s2_ss.at[u], s2_rs.at[u], to),
            put(l2_send.at[u], l2_recv.at[u], l2_ss.at[u], l2_rs.at[u], to),
        ))

    for n, u in enumerate(order):
        work(u)
        if n >= 1:
            forward(order[n - 1])

    o, m, l = gather_plane(0)
    if scatter:
        parts = [(o, m, l)]
        for u, first, second in l2_copies:
            first.wait_recv()
            second.wait_recv()
            parts.append((l2_recv[u].astype(F32), s2_recv[u, 0:1, :], s2_recv[u, 1:2, :]))
    else:
        l2_send[0] = o.astype(BF16)
        s2_send[0] = stats(m, l)
        l2_recv[hi] = o.astype(BF16)
        s2_recv[hi] = stats(m, l)
        for s in range(1, high):
            put(s2_send.at[0], s2_recv.at[hi], s2_ss.at[s], s2_rs.at[hi], line(s))
            put(l2_send.at[0], l2_recv.at[hi], l2_ss.at[s], l2_rs.at[hi], line(s))
        for s in range(1, high):
            other = lax.rem(hi + s, high)
            for src, dst, ss, rs in (
                (s2_send, s2_recv, s2_ss, s2_rs), (l2_send, l2_recv, l2_ss, l2_rs),
            ):
                pltpu.make_async_remote_copy(
                    src_ref=src.at[0], dst_ref=dst.at[other], send_sem=ss.at[s],
                    recv_sem=rs.at[other], device_id=line(s), device_id_type=MESH,
                ).wait_recv()
        parts = [
            (l2_recv[j].astype(F32), s2_recv[j, 0:1, :], s2_recv[j, 1:2, :]) for j in range(high)
        ]
    o, m, l = combine(parts, coef)
    result = o * (1.0 / l)
    mine = lo * chunk + sub_of(0) * piece
    for j in range(piece // LANES):
        at = pl.ds(pl.multiple_of(mine + j * LANES, LANES), LANES)
        out_ref[:, at] = result[:, j * LANES:(j + 1) * LANES].T.astype(BF16)

    def block(column):
        return out_ref.at[:, pl.ds(pl.multiple_of(column, LANES), piece)]

    g2_copies = []
    g1_copies = []
    if scatter:
        for s in range(1, high):
            g2_copies.append(
                (s, put(block(mine), block(mine), g2_ss.at[s], g2_rs.at[s], line(s)))
            )

    def to_plane(s, column):
        for p in (3, 1, 2):
            to = (hi * PLANE + flip(lo, p), kv)
            g1_copies.append(
                put(block(column), block(column), g1_ss.at[p, s], g1_rs.at[p, s], to)
            )

    def from_line(s):
        return lo * chunk + lax.rem(hi - s + high, high) * piece if scatter else lo * chunk

    def in_copy(ss, rs, column):
        return pltpu.make_async_remote_copy(
            src_ref=block(column), dst_ref=block(column), send_sem=ss, recv_sem=rs,
            device_id=line(1), device_id_type=MESH,
        )

    to_plane(0, mine)
    for s, _ in g2_copies:
        column = from_line(s)
        in_copy(g2_ss.at[s], g2_rs.at[s], column).wait_recv()
        to_plane(s, column)
    for s in range(subs):
        for p in (1, 2, 3):
            column = from_line(s) + (flip(lo, p) - lo) * chunk
            in_copy(g1_ss.at[p, s], g1_rs.at[p, s], column).wait_recv()
    for copy in sent:
        copy.wait_send()


def per_device(cache_keys, cache_values, importance, assignment, queries):
    shards = lax.axis_size("ctx")
    kv_size = lax.axis_size("kv")
    rows, width = cache_keys.shape
    lanes = queries.shape[1]
    high = shards // PLANE
    subs = high if (lanes // PLANE) % (high * LANES) == 0 else 1
    piece = lanes // PLANE // subs
    heads = width // LANES
    slots = 2 * NEAR + shards
    wide = 2 * width + 3 * LANES
    dma = pltpu.SemaphoreType.DMA
    vmem = pl.BlockSpec(memory_space=pltpu.VMEM)
    body = functools.partial(kernel, shards, kv_size, subs, piece)
    call = pl.pallas_call(
        body,
        out_shape=(
            jax.ShapeDtypeStruct((rows, width), BF16),
            jax.ShapeDtypeStruct((rows, width), BF16),
            jax.ShapeDtypeStruct(queries.shape, BF16),
        ),
        in_specs=[vmem] * 5,
        out_specs=(vmem,) * 3,
        scratch_shapes=[
            pltpu.VMEM((8, rows), F32),
            pltpu.VMEM((kv_size, 8, rows), F32),
            pltpu.VMEM((2, NEAR, wide), BF16),
            pltpu.VMEM((2, NEAR, wide), BF16),
            pltpu.VMEM((shards, 16, LANES), BF16),
            pltpu.VMEM((shards, 16, LANES), BF16),
            pltpu.VMEM((shards, 16, LANES), F32),
            pltpu.VMEM((slots, 2 * width + LANES), BF16),
            pltpu.VMEM((rows, 2 * width + LANES), F32),
            pltpu.VMEM((2 * LANES, lanes), BF16),
            pltpu.VMEM((heads, rows, 2 * LANES), BF16),
            pltpu.VMEM((heads, LANES + 16, rows), BF16),
            pltpu.VMEM((PLANE, subs, LANES, piece), BF16),
            pltpu.VMEM((PLANE, subs, LANES, piece), BF16),
            pltpu.VMEM((PLANE, subs, 8, piece), F32),
            pltpu.VMEM((PLANE, subs, 8, piece), F32),
            pltpu.VMEM((subs, LANES, piece), F32),
            pltpu.VMEM((subs, 8, piece), F32),
            pltpu.VMEM((high, LANES, piece), BF16),
            pltpu.VMEM((high, LANES, piece), BF16),
            pltpu.VMEM((high, 8, piece), F32),
            pltpu.VMEM((high, 8, piece), F32),
            dma((kv_size,)), dma((kv_size,)),
            dma((2,)), dma((2,)),
            dma((shards,)), dma((shards,)),
            dma((PLANE, subs)), dma((PLANE, subs)),
            dma((PLANE, subs)), dma((PLANE, subs)),
            dma((high,)), dma((high,)),
            dma((high,)), dma((high,)),
            dma((high,)), dma((high,)),
            dma((PLANE, subs)), dma((PLANE, subs)),
        ],
        compiler_params=pltpu.CompilerParams(
            collective_id=0, has_side_effects=True, vmem_limit_bytes=40 * 1024 * 1024
        ),
    )
    return call(cache_keys, cache_values, importance, assignment.reshape(1, rows), queries)


def solution(mesh):
    placed = (P("ctx", "kv"), P("ctx", "kv"), P("kv", "ctx"), P("ctx"), P(None, "kv"))
    return jax.shard_map(
        per_device,
        mesh=mesh,
        in_specs=placed,
        out_specs=(P("ctx", "kv"), P("ctx", "kv"), P(None, "kv")),
        check_vma=False,
    )
```

```python
import functools
import math

import jax
import jax.numpy as jnp
from jax import lax
from jax.experimental import pallas as pl
from jax.experimental.pallas import tpu as pltpu
from jax.sharding import PartitionSpec as P

NEAR = 16
LANES = 128
PLANE = 4
MESH = pl.DeviceIdType.MESH
F32 = jnp.float32
BF16 = jnp.bfloat16


def dot(a, b):
    return jnp.dot(a, b, preferred_element_type=F32)


def dot_t(a, b):
    return lax.dot_general(a, b, (((0,), (0,)), ((), ())), preferred_element_type=F32)


def flip(index, step):
    if step == 1:
        return index + 1 - 2 * lax.rem(index, 2)
    if step == 2:
        return index + 2 - 4 * lax.div(index, 2)
    return 3 - index


def combine(parts, coef):
    peak = functools.reduce(jnp.maximum, [m for _, m, _ in parts])
    total, weight = None, None
    for o, m, l in parts:
        factor = jnp.exp2((m - peak) * coef)
        o, l = o * factor, l * factor
        total = o if total is None else total + o
        weight = l if weight is None else weight + l
    return total, peak, weight


def stats(m, l):
    rows = lax.broadcasted_iota(jnp.int32, (8, m.shape[1]), 0)
    shape = (8, m.shape[1])
    return jnp.where(rows == 0, jnp.broadcast_to(m, shape), jnp.broadcast_to(l, shape))


def kernel(
    shards, kv_size, subs, piece,
    k_hbm, v_hbm, imp_hbm, asg_hbm, q_hbm,
    mk_ref, mv_ref, out_ref,
    k_ref, v_ref, imp_ref, asg_ref, q_ref, in_sems,
    kv_send, kv_recv, near_send, near_recv, far_send, far_recv, far_wide, arrived,
    num, q_t, k_ext, v_t,
    l1_send, l1_recv, s1_send, s1_recv, own_o, own_s,
    l2_send, l2_recv, s2_send, s2_recv,
    kv_ss, kv_rs, near_ss, near_rs, far_ss, far_rs,
    l1_ss, l1_rs, s1_ss, s1_rs, l2_ss, l2_rs, s2_ss, s2_rs,
    g2_ss, g2_rs, g1_ss, g1_rs,
):
    me = lax.axis_index("ctx")
    kv = lax.axis_index("kv")
    lo, hi = lax.rem(me, PLANE), lax.div(me, PLANE)
    high = shards // PLANE
    scatter = subs == high
    rows, width = k_ref.shape
    heads = width // LANES
    lanes = q_ref.shape[1]
    group_lanes = lanes // heads
    chunk = lanes // PLANE
    slots = 2 * NEAR + shards
    tiles = 2 * heads
    coef = math.log2(math.e) / math.sqrt(LANES)
    sent = []

    def put(src, dst, ss, rs, target):
        copy = pltpu.make_async_remote_copy(
            src_ref=src, dst_ref=dst, send_sem=ss, recv_sem=rs,
            device_id=target, device_id_type=MESH,
        )
        copy.start()
        sent.append(copy)
        return copy

    imp_in, asg_in, k_in, v_in, q_in = [
        pltpu.make_async_copy(src, dst, in_sems.at[n])
        for n, (src, dst) in enumerate((
            (imp_hbm, imp_ref), (asg_hbm, asg_ref), (k_hbm, k_ref), (v_hbm, v_ref),
            (q_hbm, q_ref),
        ))
    ]
    barrier = pltpu.get_barrier_semaphore()

    def greet(s, carry):
        pl.semaphore_signal(
            barrier, inc=1, device_id=(lax.rem(me + s, shards), kv), device_id_type=MESH
        )
        return carry

    for s in range(1, kv_size):
        pl.semaphore_signal(
            barrier, inc=1, device_id=(me, lax.rem(kv + s, kv_size)), device_id_type=MESH
        )
    lax.fori_loop(1, shards, greet, 0)
    for copy in (imp_in, asg_in, k_in, v_in, q_in):
        copy.start()

    imp_in.wait()
    part_weight = jnp.sum(imp_ref[...].astype(F32), axis=0, keepdims=True)
    kv_send[...] = jnp.broadcast_to(part_weight, (8, rows))
    for s in (0, 1, shards - 1):
        far_recv[s] = jnp.zeros((16, LANES), BF16)
    far_wide[...] = jnp.zeros_like(far_wide)

    asg_in.wait()
    asg = asg_ref[...]
    owner = jnp.right_shift(asg, rows.bit_length() - 1)
    target = jnp.bitwise_and(asg, rows - 1)
    distance = jnp.bitwise_and(owner - me, shards - 1)
    rank_row = lax.broadcasted_iota(jnp.int32, (16, rows), 0)
    distance_16 = jnp.broadcast_to(distance, (16, rows))
    wanted = jnp.where(rank_row == 0, 1, jnp.where(rank_row == 1, shards - 1, -1))
    marks = jnp.where(distance_16 == wanted, 1.0, 0.0).astype(BF16)
    earlier = jnp.where(
        lax.broadcasted_iota(jnp.int32, (rows, rows), 0)
        < lax.broadcasted_iota(jnp.int32, (rows, rows), 1),
        1.0, 0.0,
    ).astype(BF16)
    rank = dot(marks, earlier).astype(jnp.int32)
    key_next = jnp.where(distance == 1, rank[0:1], -1)
    key_prev = jnp.where(distance == shards - 1, rank[1:2], -1)
    far = jnp.where(distance >= 2, jnp.where(distance <= shards - 2, distance, -1), -1)

    def select(key, count):
        index = lax.broadcasted_iota(jnp.int32, (count, rows), 0)
        return jnp.where(jnp.broadcast_to(key, (count, rows)) == index, 1.0, 0.0)

    chosen = jnp.concatenate(
        [select(key_next, NEAR), select(key_prev, NEAR), select(far, shards)], axis=0
    )
    pl.semaphore_wait(barrier, shards - 1 + kv_size - 1)
    kv_copies = [
        put(kv_send, kv_recv.at[s], kv_ss.at[s], kv_rs.at[s], (me, lax.rem(kv + s, kv_size)))
        for s in range(1, kv_size)
    ]

    chosen_b = chosen.astype(BF16)
    k_in.wait()
    v_in.wait()
    out_rows = [dot(chosen_b, k_ref[...]), dot(chosen_b, v_ref[...])]
    meta_high = jnp.sum(
        chosen * jnp.right_shift(target, 7).astype(F32), axis=1, keepdims=True
    )
    meta_low = jnp.sum(
        chosen * jnp.bitwise_and(target, LANES - 1).astype(F32), axis=1, keepdims=True
    )
    for d in range(2):
        for part in range(2):
            near_send[d, :, part * width:(part + 1) * width] = out_rows[part][
                d * NEAR:(d + 1) * NEAR
            ].astype(BF16)
    for c in range(tiles):
        part, at = divmod(c, heads)
        far_wide[:, c, :] = out_rows[part][2 * NEAR:, at * LANES:(at + 1) * LANES]

    total_weight = part_weight
    for s, copy in enumerate(kv_copies, 1):
        copy.wait_recv()
        total_weight = total_weight + kv_recv[s, 0:1, :]
    weight = total_weight.astype(BF16).astype(F32)
    meta_weight = jnp.sum(chosen * weight, axis=1, keepdims=True)
    for m, meta in enumerate((meta_weight, meta_high, meta_low)):
        spread = jnp.broadcast_to(meta, (slots, LANES))
        for d in range(2):
            near_send[d, :, 2 * width + m * LANES:2 * width + (m + 1) * LANES] = spread[
                d * NEAR:(d + 1) * NEAR
            ].astype(BF16)
        far_wide[:, tiles + m, :] = spread[2 * NEAR:]
    far_send[...] = far_wide[...].astype(BF16)

    near_copies = [
        put(near_send.at[d], near_recv.at[d], near_ss.at[d], near_rs.at[d],
            (lax.rem(me + step, shards), kv))
        for d, step in enumerate((1, shards - 1))
    ]

    def far_copy(s):
        return pltpu.make_async_remote_copy(
            src_ref=far_send.at[s], dst_ref=far_recv.at[s],
            send_sem=far_ss.at[s], recv_sem=far_rs.at[s],
            device_id=(lax.rem(me + s, shards), kv), device_id_type=MESH,
        )

    def far_start(s, carry):
        far_copy(s).start()
        return carry

    def far_wait(s, carry):
        far_copy(s).wait()
        return carry

    lax.fori_loop(2, shards - 1, far_start, 0)

    home = jnp.where(distance == 0, target, -1)
    home_matrix = jnp.where(
        jnp.broadcast_to(home, (rows, rows))
        == lax.broadcasted_iota(jnp.int32, (rows, rows), 0),
        jnp.broadcast_to(weight, (rows, rows)), 0.0,
    ).astype(BF16)
    num[:, 0:width] = dot(home_matrix, k_ref[...])
    num[:, width:2 * width] = dot(home_matrix, v_ref[...])
    num[:, 2 * width:] = dot(home_matrix, jnp.ones((rows, LANES), BF16))
    q_in.wait()
    for j in range(lanes // LANES):
        at = slice(j * LANES, (j + 1) * LANES)
        q_t[0:LANES, at] = q_ref[:, at].T
    q_t[LANES:, :] = jnp.ones((LANES, lanes), BF16)

    for copy in near_copies:
        copy.wait_recv()
    lax.fori_loop(2, shards - 1, far_wait, 0)

    far_wide[...] = far_recv[...].astype(F32)
    for d in range(2):
        arrived[d * NEAR:(d + 1) * NEAR, 0:2 * width] = near_recv[d, :, 0:2 * width]
    for c in range(tiles):
        arrived[2 * NEAR:, c * LANES:(c + 1) * LANES] = far_wide[:, c, :].astype(BF16)
    arrived[:, 2 * width:] = jnp.ones((slots, LANES), BF16)

    def meta_of(m):
        at = slice(2 * width + m * LANES, 2 * width + (m + 1) * LANES)
        return jnp.concatenate(
            [near_recv[0, :, at].astype(F32), near_recv[1, :, at].astype(F32),
             far_wide[:, tiles + m, :]], axis=0,
        )

    in_weight = meta_of(0)
    in_target = (meta_of(1) * LANES + meta_of(2)).astype(jnp.int32)
    lane = lax.broadcasted_iota(jnp.int32, (slots, LANES), 1)
    spread_t = jnp.concatenate(
        [jnp.where(in_target == lane + b * LANES, in_weight, 0.0) for b in range(rows // LANES)],
        axis=1,
    ).astype(BF16)

    denominator = num[:, 2 * width:] + dot_t(spread_t, arrived[:, 2 * width:])
    kept = denominator > 0.0
    inverse = 1.0 / jnp.where(kept, denominator, 1.0)
    first_lane = lax.broadcasted_iota(jnp.int32, (rows, LANES), 1) == 0
    bias = jnp.where(first_lane, jnp.where(kept, 0.0, -1e30), 0.0).astype(BF16)
    for h in range(heads):
        at = slice(h * LANES, (h + 1) * LANES)
        far_at = slice(width + h * LANES, width + (h + 1) * LANES)
        key = (num[:, at] + dot_t(spread_t, arrived[:, at])) * inverse
        key = jnp.where(kept, key, k_ref[:, at].astype(F32)).astype(BF16)
        mk_ref[:, at] = key
        k_ext[h, :, 0:LANES] = key
        k_ext[h, :, LANES:] = bias
        value = (num[:, far_at] + dot_t(spread_t, arrived[:, far_at])) * inverse
        value = jnp.where(kept, value, v_ref[:, at].astype(F32)).astype(BF16)
        mv_ref[:, at] = value
        v_t[h, 0:LANES, :] = value.T
        v_t[h, LANES:, :] = jnp.ones((16, rows), BF16)

    def attend(column):
        h = lax.div(column, group_lanes)
        queries = q_t[:, pl.ds(pl.multiple_of(column, LANES), piece)]
        score = dot(k_ext[h], queries)
        peak = jnp.max(score, axis=0, keepdims=True)
        prob = jnp.exp2((score - peak) * coef).astype(BF16)
        both = dot(v_t[h], prob)
        return both[0:LANES], peak, both[LANES:LANES + 1]

    def sub_of(u):
        return lax.rem(hi + u, high) if scatter else 0

    order = list(range(1, subs)) + [0]
    l1_copies = {}

    def work(u):
        for s in (3, 1, 2, 0):
            dest = flip(lo, s) if s else lo
            o, m, l = attend(dest * chunk + sub_of(u) * piece)
            if s == 0:
                own_o[u] = o
                own_s[u] = stats(m, l)
                continue
            l1_send[s, u] = o.astype(BF16)
            s1_send[s, u] = stats(m, l)
            to = (hi * PLANE + dest, kv)
            l1_copies[s, u] = (
                put(s1_send.at[s, u], s1_recv.at[s, u], s1_ss.at[s, u], s1_rs.at[s, u], to),
                put(l1_send.at[s, u], l1_recv.at[s, u], l1_ss.at[s, u], l1_rs.at[s, u], to),
            )

    def gather_plane(u):
        parts = [(own_o[u], own_s[u, 0:1, :], own_s[u, 1:2, :])]
        for s in (1, 2, 3):
            for copy in l1_copies[s, u]:
                copy.wait_recv()
            parts.append(
                (l1_recv[s, u].astype(F32), s1_recv[s, u, 0:1, :], s1_recv[s, u, 1:2, :])
            )
        return combine(parts, coef)

    def line(s):
        return (lax.rem(hi + s, high) * PLANE + lo, kv)

    l2_copies = []

    def forward(u):
        o, m, l = gather_plane(u)
        l2_send[u] = o.astype(BF16)
        s2_send[u] = stats(m, l)
        to = line(u)
        l2_copies.append((
            u,
            put(s2_send.at[u], s2_recv.at[u], s2_ss.at[u], s2_rs.at[u], to),
            put(l2_send.at[u], l2_recv.at[u], l2_ss.at[u], l2_rs.at[u], to),
        ))

    for n, u in enumerate(order):
        work(u)
        if n >= 1:
            forward(order[n - 1])

    o, m, l = gather_plane(0)
    if scatter:
        parts = [(o, m, l)]
        for u, first, second in l2_copies:
            first.wait_recv()
            second.wait_recv()
            parts.append((l2_recv[u].astype(F32), s2_recv[u, 0:1, :], s2_recv[u, 1:2, :]))
    else:
        l2_send[0] = o.astype(BF16)
        s2_send[0] = stats(m, l)
        l2_recv[hi] = o.astype(BF16)
        s2_recv[hi] = stats(m, l)
        for s in range(1, high):
            put(s2_send.at[0], s2_recv.at[hi], s2_ss.at[s], s2_rs.at[hi], line(s))
            put(l2_send.at[0], l2_recv.at[hi], l2_ss.at[s], l2_rs.at[hi], line(s))
        for s in range(1, high):
            other = lax.rem(hi + s, high)
            for src, dst, ss, rs in (
                (s2_send, s2_recv, s2_ss, s2_rs), (l2_send, l2_recv, l2_ss, l2_rs),
            ):
                pltpu.make_async_remote_copy(
                    src_ref=src.at[0], dst_ref=dst.at[other], send_sem=ss.at[s],
                    recv_sem=rs.at[other], device_id=line(s), device_id_type=MESH,
                ).wait_recv()
        parts = [
            (l2_recv[j].astype(F32), s2_recv[j, 0:1, :], s2_recv[j, 1:2, :]) for j in range(high)
        ]
    o, m, l = combine(parts, coef)
    result = o * (1.0 / l)
    mine = lo * chunk + sub_of(0) * piece
    for j in range(piece // LANES):
        at = pl.ds(pl.multiple_of(mine + j * LANES, LANES), LANES)
        out_ref[:, at] = result[:, j * LANES:(j + 1) * LANES].T.astype(BF16)

    def block(column):
        return out_ref.at[:, pl.ds(pl.multiple_of(column, LANES), piece)]

    if scatter:
        for s in range(1, high):
            put(block(mine), block(mine), g2_ss.at[s], g2_rs.at[s], line(s))

    half = piece // 2

    def part(column, h):
        return out_ref.at[:, pl.ds(pl.multiple_of(column + h * half, LANES), half)]

    across = {p: (hi * PLANE + flip(lo, p), kv) for p in (1, 2)}

    def from_line(s):
        return lo * chunk + lax.rem(hi - s + high, high) * piece if scatter else lo * chunk

    def beside(s, p):
        return from_line(s) + (flip(lo, p) - lo) * chunk

    def await_copy(view, ss, rs):
        pltpu.make_async_remote_copy(
            src_ref=view, dst_ref=view, send_sem=ss, recv_sem=rs,
            device_id=line(1), device_id_type=MESH,
        ).wait_recv()

    def to_plane(s):
        view = block(from_line(s))
        for p in (1, 2):
            put(view, view, g1_ss.at[p, s], g1_rs.at[p, s], across[p])

    def pass_on(s):
        for p, h, over, slot in ((1, 0, 2, 3), (2, 1, 1, 0)):
            await_copy(block(beside(s, p)), g1_ss.at[p, s], g1_rs.at[p, s])
            view = part(beside(s, p), h)
            put(view, view, g1_ss.at[slot, s], g1_rs.at[slot, s], across[over])

    to_plane(0)
    for s in range(1, subs):
        await_copy(block(from_line(s)), g2_ss.at[s], g2_rs.at[s])
        to_plane(s)
        pass_on(s - 1)
    pass_on(subs - 1)
    for s in range(subs):
        for h, slot in ((0, 3), (1, 0)):
            await_copy(part(beside(s, 3), h), g1_ss.at[slot, s], g1_rs.at[slot, s])
    for copy in sent:
        copy.wait_send()


def write_out(mk_ref, mv_ref, out_ref, mk_hbm, mv_hbm, out_hbm, sems):
    copies = [
        pltpu.make_async_copy(src, dst, sems.at[n])
        for n, (src, dst) in enumerate(((out_ref, out_hbm), (mk_ref, mk_hbm), (mv_ref, mv_hbm)))
    ]
    for copy in copies:
        copy.start()
    for copy in copies:
        copy.wait()


def per_device(cache_keys, cache_values, importance, assignment, queries):
    shards = lax.axis_size("ctx")
    kv_size = lax.axis_size("kv")
    rows, width = cache_keys.shape
    lanes = queries.shape[1]
    high = shards // PLANE
    subs = high if (lanes // PLANE) % (high * LANES) == 0 else 1
    piece = lanes // PLANE // subs
    heads = width // LANES
    slots = 2 * NEAR + shards
    wide = 2 * width + 3 * LANES
    dma = pltpu.SemaphoreType.DMA
    vmem = pl.BlockSpec(memory_space=pltpu.VMEM)
    hbm = pl.BlockSpec(memory_space=pltpu.HBM)
    body = functools.partial(kernel, shards, kv_size, subs, piece)
    shapes = (
        jax.ShapeDtypeStruct((rows, width), BF16),
        jax.ShapeDtypeStruct((rows, width), BF16),
        jax.ShapeDtypeStruct(queries.shape, BF16),
    )
    call = pl.pallas_call(
        body,
        out_shape=tuple(pltpu.VMEM(x.shape, x.dtype) for x in shapes),
        in_specs=[hbm] * 5,
        out_specs=(vmem,) * 3,
        scratch_shapes=[
            pltpu.VMEM((rows, width), BF16),
            pltpu.VMEM((rows, width), BF16),
            pltpu.VMEM(importance.shape, BF16),
            pltpu.VMEM((1, rows), jnp.int32),
            pltpu.VMEM(queries.shape, BF16),
            dma((5,)),
            pltpu.VMEM((8, rows), F32),
            pltpu.VMEM((kv_size, 8, rows), F32),
            pltpu.VMEM((2, NEAR, wide), BF16),
            pltpu.VMEM((2, NEAR, wide), BF16),
            pltpu.VMEM((shards, 16, LANES), BF16),
            pltpu.VMEM((shards, 16, LANES), BF16),
            pltpu.VMEM((shards, 16, LANES), F32),
            pltpu.VMEM((slots, 2 * width + LANES), BF16),
            pltpu.VMEM((rows, 2 * width + LANES), F32),
            pltpu.VMEM((2 * LANES, lanes), BF16),
            pltpu.VMEM((heads, rows, 2 * LANES), BF16),
            pltpu.VMEM((heads, LANES + 16, rows), BF16),
            pltpu.VMEM((PLANE, subs, LANES, piece), BF16),
            pltpu.VMEM((PLANE, subs, LANES, piece), BF16),
            pltpu.VMEM((PLANE, subs, 8, piece), F32),
            pltpu.VMEM((PLANE, subs, 8, piece), F32),
            pltpu.VMEM((subs, LANES, piece), F32),
            pltpu.VMEM((subs, 8, piece), F32),
            pltpu.VMEM((high, LANES, piece), BF16),
            pltpu.VMEM((high, LANES, piece), BF16),
            pltpu.VMEM((high, 8, piece), F32),
            pltpu.VMEM((high, 8, piece), F32),
            dma((kv_size,)), dma((kv_size,)),
            dma((2,)), dma((2,)),
            dma((shards,)), dma((shards,)),
            dma((PLANE, subs)), dma((PLANE, subs)),
            dma((PLANE, subs)), dma((PLANE, subs)),
            dma((high,)), dma((high,)),
            dma((high,)), dma((high,)),
            dma((high,)), dma((high,)),
            dma((PLANE, subs)), dma((PLANE, subs)),
        ],
        compiler_params=pltpu.CompilerParams(
            collective_id=0, has_side_effects=True, vmem_limit_bytes=40 * 1024 * 1024
        ),
    )
    operands = (cache_keys, cache_values, importance, assignment.reshape(1, rows), queries)
    results = call(*(pltpu.with_memory_space_constraint(x, pltpu.HBM) for x in operands))
    return pl.pallas_call(
        write_out,
        out_shape=shapes,
        in_specs=[vmem] * 3,
        out_specs=(hbm,) * 3,
        scratch_shapes=[dma((3,))],
    )(*results)


def solution(mesh):
    placed = (P("ctx", "kv"), P("ctx", "kv"), P("kv", "ctx"), P("ctx"), P(None, "kv"))
    return jax.shard_map(
        per_device,
        mesh=mesh,
        in_specs=placed,
        out_specs=(P("ctx", "kv"), P("ctx", "kv"), P(None, "kv")),
        check_vma=False,
    )
```

```python
import functools
import math

import jax
import jax.numpy as jnp
from jax import lax
from jax.experimental import pallas as pl
from jax.experimental.pallas import tpu as pltpu
from jax.sharding import PartitionSpec as P

NEAR = 16
LANES = 128
PLANE = 4
MESH = pl.DeviceIdType.MESH
F32 = jnp.float32
BF16 = jnp.bfloat16


def dot(a, b):
    return jnp.dot(a, b, preferred_element_type=F32)


def dot_t(a, b):
    return lax.dot_general(a, b, (((0,), (0,)), ((), ())), preferred_element_type=F32)


def flip(index, step):
    if step == 1:
        return index + 1 - 2 * lax.rem(index, 2)
    if step == 2:
        return index + 2 - 4 * lax.div(index, 2)
    return 3 - index


def combine(parts, coef):
    peak = functools.reduce(jnp.maximum, [m for _, m, _ in parts])
    total, weight = None, None
    for o, m, l in parts:
        factor = jnp.exp2((m - peak) * coef)
        o, l = o * factor, l * factor
        total = o if total is None else total + o
        weight = l if weight is None else weight + l
    return total, peak, weight


def stats(m, l):
    rows = lax.broadcasted_iota(jnp.int32, (8, m.shape[1]), 0)
    shape = (8, m.shape[1])
    return jnp.where(rows == 0, jnp.broadcast_to(m, shape), jnp.broadcast_to(l, shape))


def kernel(
    shards, kv_size, subs, piece,
    k_hbm, v_hbm, imp_hbm, asg_hbm, q_hbm,
    mk_ref, mv_ref, out_ref,
    k_ref, v_ref, imp_ref, asg_ref, q_ref, in_sems,
    kv_send, kv_recv, near_send, near_recv, far_send, far_recv, far_wide, arrived,
    num, q_t, k_ext, v_t,
    l1_send, l1_recv, s1_send, s1_recv, h1_send, h1_recv, t1_send, t1_recv, own_o, own_s,
    l2_send, l2_recv, s2_send, s2_recv,
    kv_ss, kv_rs, near_ss, near_rs, far_ss, far_rs,
    l1_ss, l1_rs, s1_ss, s1_rs, h1_ss, h1_rs, t1_ss, t1_rs, l2_ss, l2_rs, s2_ss, s2_rs,
    g2_ss, g2_rs, g1_ss, g1_rs,
):
    me = lax.axis_index("ctx")
    kv = lax.axis_index("kv")
    lo, hi = lax.rem(me, PLANE), lax.div(me, PLANE)
    high = shards // PLANE
    scatter = subs == high
    rows, width = k_ref.shape
    heads = width // LANES
    lanes = q_ref.shape[1]
    group_lanes = lanes // heads
    chunk = lanes // PLANE
    slots = 2 * NEAR + shards
    tiles = 2 * heads
    coef = math.log2(math.e) / math.sqrt(LANES)
    half = piece // 2
    sent = []

    def put(src, dst, ss, rs, target):
        copy = pltpu.make_async_remote_copy(
            src_ref=src, dst_ref=dst, send_sem=ss, recv_sem=rs,
            device_id=target, device_id_type=MESH,
        )
        copy.start()
        sent.append(copy)
        return copy

    imp_in, asg_in, k_in, v_in, q_in = [
        pltpu.make_async_copy(src, dst, in_sems.at[n])
        for n, (src, dst) in enumerate((
            (imp_hbm, imp_ref), (asg_hbm, asg_ref), (k_hbm, k_ref), (v_hbm, v_ref),
            (q_hbm, q_ref),
        ))
    ]
    barrier = pltpu.get_barrier_semaphore()

    def greet(s, carry):
        pl.semaphore_signal(
            barrier, inc=1, device_id=(lax.rem(me + s, shards), kv), device_id_type=MESH
        )
        return carry

    for s in range(1, kv_size):
        pl.semaphore_signal(
            barrier, inc=1, device_id=(me, lax.rem(kv + s, kv_size)), device_id_type=MESH
        )
    lax.fori_loop(1, shards, greet, 0)
    for copy in (imp_in, asg_in, k_in, v_in, q_in):
        copy.start()

    imp_in.wait()
    part_weight = jnp.sum(imp_ref[...].astype(F32), axis=0, keepdims=True)
    kv_send[...] = jnp.broadcast_to(part_weight, (8, rows))
    for s in (0, 1, shards - 1):
        far_recv[s] = jnp.zeros((16, LANES), BF16)
    far_wide[...] = jnp.zeros_like(far_wide)

    asg_in.wait()
    asg = asg_ref[...]
    owner = jnp.right_shift(asg, rows.bit_length() - 1)
    target = jnp.bitwise_and(asg, rows - 1)
    distance = jnp.bitwise_and(owner - me, shards - 1)
    rank_row = lax.broadcasted_iota(jnp.int32, (16, rows), 0)
    distance_16 = jnp.broadcast_to(distance, (16, rows))
    wanted = jnp.where(rank_row == 0, 1, jnp.where(rank_row == 1, shards - 1, -1))
    marks = jnp.where(distance_16 == wanted, 1.0, 0.0).astype(BF16)
    earlier = jnp.where(
        lax.broadcasted_iota(jnp.int32, (rows, rows), 0)
        < lax.broadcasted_iota(jnp.int32, (rows, rows), 1),
        1.0, 0.0,
    ).astype(BF16)
    rank = dot(marks, earlier).astype(jnp.int32)
    key_next = jnp.where(distance == 1, rank[0:1], -1)
    key_prev = jnp.where(distance == shards - 1, rank[1:2], -1)
    far = jnp.where(distance >= 2, jnp.where(distance <= shards - 2, distance, -1), -1)

    def select(key, count):
        index = lax.broadcasted_iota(jnp.int32, (count, rows), 0)
        return jnp.where(jnp.broadcast_to(key, (count, rows)) == index, 1.0, 0.0)

    chosen = jnp.concatenate(
        [select(key_next, NEAR), select(key_prev, NEAR), select(far, shards)], axis=0
    )
    pl.semaphore_wait(barrier, shards - 1 + kv_size - 1)
    kv_copies = [
        put(kv_send, kv_recv.at[s], kv_ss.at[s], kv_rs.at[s], (me, lax.rem(kv + s, kv_size)))
        for s in range(1, kv_size)
    ]

    chosen_b = chosen.astype(BF16)
    k_in.wait()
    v_in.wait()
    out_rows = [dot(chosen_b, k_ref[...]), dot(chosen_b, v_ref[...])]
    meta_high = jnp.sum(
        chosen * jnp.right_shift(target, 7).astype(F32), axis=1, keepdims=True
    )
    meta_low = jnp.sum(
        chosen * jnp.bitwise_and(target, LANES - 1).astype(F32), axis=1, keepdims=True
    )
    for d in range(2):
        for part in range(2):
            near_send[d, :, part * width:(part + 1) * width] = out_rows[part][
                d * NEAR:(d + 1) * NEAR
            ].astype(BF16)
    for c in range(tiles):
        part, at = divmod(c, heads)
        far_wide[:, c, :] = out_rows[part][2 * NEAR:, at * LANES:(at + 1) * LANES]

    total_weight = part_weight
    for s, copy in enumerate(kv_copies, 1):
        copy.wait_recv()
        total_weight = total_weight + kv_recv[s, 0:1, :]
    weight = total_weight.astype(BF16).astype(F32)
    meta_weight = jnp.sum(chosen * weight, axis=1, keepdims=True)
    for m, meta in enumerate((meta_weight, meta_high, meta_low)):
        spread = jnp.broadcast_to(meta, (slots, LANES))
        for d in range(2):
            near_send[d, :, 2 * width + m * LANES:2 * width + (m + 1) * LANES] = spread[
                d * NEAR:(d + 1) * NEAR
            ].astype(BF16)
        far_wide[:, tiles + m, :] = spread[2 * NEAR:]
    far_send[...] = far_wide[...].astype(BF16)

    near_copies = [
        put(near_send.at[d], near_recv.at[d], near_ss.at[d], near_rs.at[d],
            (lax.rem(me + step, shards), kv))
        for d, step in enumerate((1, shards - 1))
    ]

    def far_copy(s):
        return pltpu.make_async_remote_copy(
            src_ref=far_send.at[s], dst_ref=far_recv.at[s],
            send_sem=far_ss.at[s], recv_sem=far_rs.at[s],
            device_id=(lax.rem(me + s, shards), kv), device_id_type=MESH,
        )

    def far_start(s, carry):
        far_copy(s).start()
        return carry

    def far_wait(s, carry):
        far_copy(s).wait()
        return carry

    lax.fori_loop(2, shards - 1, far_start, 0)

    home = jnp.where(distance == 0, target, -1)
    home_matrix = jnp.where(
        jnp.broadcast_to(home, (rows, rows))
        == lax.broadcasted_iota(jnp.int32, (rows, rows), 0),
        jnp.broadcast_to(weight, (rows, rows)), 0.0,
    ).astype(BF16)
    num[:, 0:width] = dot(home_matrix, k_ref[...])
    num[:, width:2 * width] = dot(home_matrix, v_ref[...])
    num[:, 2 * width:] = dot(home_matrix, jnp.ones((rows, LANES), BF16))
    q_in.wait()

    def turn_queries(j, carry):
        at = pl.ds(pl.multiple_of(j * 2 * LANES, 2 * LANES), 2 * LANES)
        block = q_ref[:, at]
        q_t[0:LANES, at] = jnp.concatenate([block[:, 0:LANES].T, block[:, LANES:].T], axis=1)
        return carry

    lax.fori_loop(0, lanes // (2 * LANES), turn_queries, 0)
    q_t[LANES:, :] = jnp.ones((LANES, lanes), BF16)

    for copy in near_copies:
        copy.wait_recv()
    lax.fori_loop(2, shards - 1, far_wait, 0)

    far_wide[...] = far_recv[...].astype(F32)
    for d in range(2):
        arrived[d * NEAR:(d + 1) * NEAR, 0:2 * width] = near_recv[d, :, 0:2 * width]
    for c in range(tiles):
        arrived[2 * NEAR:, c * LANES:(c + 1) * LANES] = far_wide[:, c, :].astype(BF16)
    arrived[:, 2 * width:] = jnp.ones((slots, LANES), BF16)

    def meta_of(m):
        at = slice(2 * width + m * LANES, 2 * width + (m + 1) * LANES)
        return jnp.concatenate(
            [near_recv[0, :, at].astype(F32), near_recv[1, :, at].astype(F32),
             far_wide[:, tiles + m, :]], axis=0,
        )

    in_weight = meta_of(0)
    in_target = (meta_of(1) * LANES + meta_of(2)).astype(jnp.int32)
    lane = lax.broadcasted_iota(jnp.int32, (slots, LANES), 1)
    spread_t = jnp.concatenate(
        [jnp.where(in_target == lane + b * LANES, in_weight, 0.0) for b in range(rows // LANES)],
        axis=1,
    ).astype(BF16)

    denominator = num[:, 2 * width:] + dot_t(spread_t, arrived[:, 2 * width:])
    kept = denominator > 0.0
    inverse = 1.0 / jnp.where(kept, denominator, 1.0)
    first_lane = lax.broadcasted_iota(jnp.int32, (rows, LANES), 1) == 0
    bias = jnp.where(first_lane, jnp.where(kept, 0.0, -1e30), 0.0).astype(BF16)
    for h in range(heads):
        at = slice(h * LANES, (h + 1) * LANES)
        far_at = slice(width + h * LANES, width + (h + 1) * LANES)
        key = (num[:, at] + dot_t(spread_t, arrived[:, at])) * inverse
        key = jnp.where(kept, key, k_ref[:, at].astype(F32)).astype(BF16)
        mk_ref[:, at] = key
        k_ext[h, :, 0:LANES] = key
        k_ext[h, :, LANES:] = bias
        value = (num[:, far_at] + dot_t(spread_t, arrived[:, far_at])) * inverse
        value = jnp.where(kept, value, v_ref[:, at].astype(F32)).astype(BF16)
        mv_ref[:, at] = value
        v_t[h, 0:LANES, :] = value.T
        v_t[h, LANES:, :] = jnp.ones((16, rows), BF16)

    def attend(column):
        h = lax.div(column, group_lanes)
        queries = q_t[:, pl.ds(pl.multiple_of(column, LANES), piece)]
        score = dot(k_ext[h], queries)
        peak = jnp.max(score, axis=0, keepdims=True)
        prob = jnp.exp2((score - peak) * coef).astype(BF16)
        both = dot(v_t[h], prob)
        return both[0:LANES], peak, both[LANES:LANES + 1]

    def sub_of(u):
        return lax.rem(hi + u, high) if scatter else 0

    across = {p: (hi * PLANE + flip(lo, p), kv) for p in (1, 2)}
    halves = (slice(0, half), slice(half, piece))

    def hop_one(p, u):
        return [
            pltpu.make_async_remote_copy(
                src_ref=src.at[p, u], dst_ref=dst.at[p, u], send_sem=ss.at[p, u],
                recv_sem=rs.at[p, u], device_id=across[p], device_id_type=MESH,
            )
            for src, dst, ss, rs in (
                (s1_send, s1_recv, s1_ss, s1_rs), (l1_send, l1_recv, l1_ss, l1_rs),
            )
        ]

    def hop_two(p, u):
        return [
            pltpu.make_async_remote_copy(
                src_ref=src.at[p, u], dst_ref=dst.at[p, u], send_sem=ss.at[p, u],
                recv_sem=rs.at[p, u], device_id=across[p], device_id_type=MESH,
            )
            for src, dst, ss, rs in (
                (t1_send, t1_recv, t1_ss, t1_rs), (h1_send, h1_recv, h1_ss, h1_rs),
            )
        ]

    def hop_line(u):
        return [
            pltpu.make_async_remote_copy(
                src_ref=src.at[u], dst_ref=dst.at[u], send_sem=ss.at[u],
                recv_sem=rs.at[u], device_id=line(u), device_id_type=MESH,
            )
            for src, dst, ss, rs in (
                (s2_send, s2_recv, s2_ss, s2_rs), (l2_send, l2_recv, l2_ss, l2_rs),
            )
        ]

    def line(s):
        return (lax.rem(hi + s, high) * PLANE + lo, kv)

    def begin(copies):
        for copy in copies:
            copy.start()

    def work(u):
        for s in (3, 1, 2, 0):
            dest = flip(lo, s) if s else lo
            o, m, l = attend(dest * chunk + sub_of(u) * piece)
            st = stats(m, l)
            if s == 3:
                for p, h in ((1, 0), (2, 1)):
                    l1_send[p, u, :, halves[0]] = o[:, halves[h]].astype(BF16)
                    s1_send[p, u, :, halves[0]] = st[:, halves[h]]
            elif s == 0:
                own_o[0, u] = o
                own_s[0, u] = st
            else:
                out, stay = (0, 1) if s == 1 else (1, 0)
                l1_send[s, u, :, halves[1]] = o[:, halves[out]].astype(BF16)
                s1_send[s, u, :, halves[1]] = st[:, halves[out]]
                begin(hop_one(s, u))
                own_o[s, u, :, halves[0]] = o[:, halves[stay]]
                own_s[s, u, :, halves[0]] = st[:, halves[stay]]

    def triple(data, extra, u, p, at):
        return (
            data[p, u, :, at].astype(F32), extra[p, u, 0:1, at], extra[p, u, 1:2, at]
        )

    def relay(u):
        for p in (1, 2):
            for copy in hop_one(p, u):
                copy.wait_recv()
        for p in (1, 2):
            o, m, l = combine(
                [triple(own_o, own_s, u, 3 - p, halves[0]),
                 triple(l1_recv, s1_recv, u, p, halves[0])], coef,
            )
            h1_send[3 - p, u] = o.astype(BF16)
            t1_send[3 - p, u] = stats(m, l)
            begin(hop_two(3 - p, u))

    def gather_plane(u):
        for p in (1, 2):
            for copy in hop_two(p, u):
                copy.wait_recv()
        sides = []
        for p in (1, 2):
            sides.append(combine(
                [triple(own_o, own_s, u, 0, halves[p - 1]),
                 triple(l1_recv, s1_recv, u, p, halves[1]),
                 triple(h1_recv, t1_recv, u, 3 - p, slice(0, half))], coef,
            ))
        return [jnp.concatenate(pair, axis=1) for pair in zip(*sides)]

    def forward(u):
        o, m, l = gather_plane(u)
        l2_send[u] = o.astype(BF16)
        s2_send[u] = stats(m, l)
        begin(hop_line(u))

    def turn(n, carry):
        work(lax.rem(n + 1, subs))

        @pl.when(n >= 1)
        def _():
            relay(n)

        @pl.when(n >= 2)
        def _():
            forward(n - 1)

        return carry

    lax.fori_loop(0, subs, turn, 0)
    relay(0)
    if scatter:
        forward(subs - 1)
    o, m, l = gather_plane(0)
    if scatter:
        parts = [(o, m, l)]
        for u in range(1, high):
            for copy in hop_line(u):
                copy.wait_recv()
            parts.append((l2_recv[u].astype(F32), s2_recv[u, 0:1, :], s2_recv[u, 1:2, :]))
    else:
        l2_send[0] = o.astype(BF16)
        s2_send[0] = stats(m, l)
        l2_recv[hi] = o.astype(BF16)
        s2_recv[hi] = stats(m, l)
        for s in range(1, high):
            put(s2_send.at[0], s2_recv.at[hi], s2_ss.at[s], s2_rs.at[hi], line(s))
            put(l2_send.at[0], l2_recv.at[hi], l2_ss.at[s], l2_rs.at[hi], line(s))
        for s in range(1, high):
            other = lax.rem(hi + s, high)
            for src, dst, ss, rs in (
                (s2_send, s2_recv, s2_ss, s2_rs), (l2_send, l2_recv, l2_ss, l2_rs),
            ):
                pltpu.make_async_remote_copy(
                    src_ref=src.at[0], dst_ref=dst.at[other], send_sem=ss.at[s],
                    recv_sem=rs.at[other], device_id=line(s), device_id_type=MESH,
                ).wait_recv()
        parts = [
            (l2_recv[j].astype(F32), s2_recv[j, 0:1, :], s2_recv[j, 1:2, :]) for j in range(high)
        ]
    o, m, l = combine(parts, coef)
    result = o * (1.0 / l)
    mine = lo * chunk + sub_of(0) * piece
    for j in range(piece // LANES):
        at = pl.ds(pl.multiple_of(mine + j * LANES, LANES), LANES)
        out_ref[:, at] = result[:, j * LANES:(j + 1) * LANES].T.astype(BF16)

    def block(column):
        return out_ref.at[:, pl.ds(pl.multiple_of(column, LANES), piece)]

    if scatter:
        for s in range(1, high):
            put(block(mine), block(mine), g2_ss.at[s], g2_rs.at[s], line(s))

    def part(column, h):
        return out_ref.at[:, pl.ds(pl.multiple_of(column + h * half, LANES), half)]

    def from_line(s):
        return lo * chunk + lax.rem(hi - s + high, high) * piece if scatter else lo * chunk

    def beside(s, p):
        return from_line(s) + (flip(lo, p) - lo) * chunk

    def await_copy(view, ss, rs):
        pltpu.make_async_remote_copy(
            src_ref=view, dst_ref=view, send_sem=ss, recv_sem=rs,
            device_id=line(1), device_id_type=MESH,
        ).wait_recv()

    def to_plane(s):
        view = block(from_line(s))
        for p in (1, 2):
            put(view, view, g1_ss.at[p, s], g1_rs.at[p, s], across[p])

    def pass_on(s):
        for p, h, over, slot in ((1, 0, 2, 3), (2, 1, 1, 0)):
            await_copy(block(beside(s, p)), g1_ss.at[p, s], g1_rs.at[p, s])
            view = part(beside(s, p), h)
            put(view, view, g1_ss.at[slot, s], g1_rs.at[slot, s], across[over])

    to_plane(0)
    for s in range(1, subs):
        await_copy(block(from_line(s)), g2_ss.at[s], g2_rs.at[s])
        to_plane(s)
        pass_on(s - 1)
    pass_on(subs - 1)
    for s in range(subs):
        for h, slot in ((0, 3), (1, 0)):
            await_copy(part(beside(s, 3), h), g1_ss.at[slot, s], g1_rs.at[slot, s])
    for copy in sent:
        copy.wait_send()

    def finish(u, carry):
        for p in (1, 2):
            for copy in hop_one(p, u) + hop_two(p, u):
                copy.wait_send()
        if scatter:
            @pl.when(u >= 1)
            def _():
                for copy in hop_line(u):
                    copy.wait_send()
        return carry

    lax.fori_loop(0, subs, finish, 0)


def per_device(cache_keys, cache_values, importance, assignment, queries):
    shards = lax.axis_size("ctx")
    kv_size = lax.axis_size("kv")
    rows, width = cache_keys.shape
    lanes = queries.shape[1]
    high = shards // PLANE
    subs = high if (lanes // PLANE) % (high * LANES) == 0 else 1
    piece = lanes // PLANE // subs
    heads = width // LANES
    slots = 2 * NEAR + shards
    wide = 2 * width + 3 * LANES
    dma = pltpu.SemaphoreType.DMA
    vmem = pl.BlockSpec(memory_space=pltpu.VMEM)
    hbm = pl.BlockSpec(memory_space=pltpu.HBM)
    body = functools.partial(kernel, shards, kv_size, subs, piece)
    shapes = (
        jax.ShapeDtypeStruct((rows, width), BF16),
        jax.ShapeDtypeStruct((rows, width), BF16),
        jax.ShapeDtypeStruct(queries.shape, BF16),
    )
    call = pl.pallas_call(
        body,
        out_shape=tuple(pltpu.VMEM(x.shape, x.dtype) for x in shapes),
        in_specs=[hbm] * 5,
        out_specs=(vmem,) * 3,
        scratch_shapes=[
            pltpu.VMEM((rows, width), BF16),
            pltpu.VMEM((rows, width), BF16),
            pltpu.VMEM(importance.shape, BF16),
            pltpu.VMEM((1, rows), jnp.int32),
            pltpu.VMEM(queries.shape, BF16),
            dma((5,)),
            pltpu.VMEM((8, rows), F32),
            pltpu.VMEM((kv_size, 8, rows), F32),
            pltpu.VMEM((2, NEAR, wide), BF16),
            pltpu.VMEM((2, NEAR, wide), BF16),
            pltpu.VMEM((shards, 16, LANES), BF16),
            pltpu.VMEM((shards, 16, LANES), BF16),
            pltpu.VMEM((shards, 16, LANES), F32),
            pltpu.VMEM((slots, 2 * width + LANES), BF16),
            pltpu.VMEM((rows, 2 * width + LANES), F32),
            pltpu.VMEM((2 * LANES, lanes), BF16),
            pltpu.VMEM((heads, rows, 2 * LANES), BF16),
            pltpu.VMEM((heads, LANES + 16, rows), BF16),
            pltpu.VMEM((3, subs, LANES, piece), BF16),
            pltpu.VMEM((3, subs, LANES, piece), BF16),
            pltpu.VMEM((3, subs, 8, piece), F32),
            pltpu.VMEM((3, subs, 8, piece), F32),
            pltpu.VMEM((3, subs, LANES, piece // 2), BF16),
            pltpu.VMEM((3, subs, LANES, piece // 2), BF16),
            pltpu.VMEM((3, subs, 8, piece // 2), F32),
            pltpu.VMEM((3, subs, 8, piece // 2), F32),
            pltpu.VMEM((3, subs, LANES, piece), F32),
            pltpu.VMEM((3, subs, 8, piece), F32),
            pltpu.VMEM((high, LANES, piece), BF16),
            pltpu.VMEM((high, LANES, piece), BF16),
            pltpu.VMEM((high, 8, piece), F32),
            pltpu.VMEM((high, 8, piece), F32),
            dma((kv_size,)), dma((kv_size,)),
            dma((2,)), dma((2,)),
            dma((shards,)), dma((shards,)),
            dma((3, subs)), dma((3, subs)),
            dma((3, subs)), dma((3, subs)),
            dma((3, subs)), dma((3, subs)),
            dma((3, subs)), dma((3, subs)),
            dma((high,)), dma((high,)),
            dma((high,)), dma((high,)),
            dma((high,)), dma((high,)),
            dma((PLANE, subs)), dma((PLANE, subs)),
        ],
        compiler_params=pltpu.CompilerParams(
            collective_id=0, has_side_effects=True, vmem_limit_bytes=40 * 1024 * 1024
        ),
    )
    operands = (cache_keys, cache_values, importance, assignment.reshape(1, rows), queries)
    return call(*(pltpu.with_memory_space_constraint(x, pltpu.HBM) for x in operands))


def solution(mesh):
    placed = (P("ctx", "kv"), P("ctx", "kv"), P("kv", "ctx"), P("ctx"), P(None, "kv"))
    return jax.shard_map(
        per_device,
        mesh=mesh,
        in_specs=placed,
        out_specs=(P("ctx", "kv"), P("ctx", "kv"), P(None, "kv")),
        check_vma=False,
    )
```

```python
import functools
import math

import jax
import jax.numpy as jnp
from jax import lax
from jax.experimental import pallas as pl
from jax.experimental.pallas import tpu as pltpu
from jax.sharding import PartitionSpec as P

NEAR = 16
LANES = 128
PLANE = 4
MESH = pl.DeviceIdType.MESH
F32 = jnp.float32
BF16 = jnp.bfloat16


def dot(a, b):
    return jnp.dot(a, b, preferred_element_type=F32)


def dot_t(a, b):
    return lax.dot_general(a, b, (((0,), (0,)), ((), ())), preferred_element_type=F32)


def flip(index, step):
    if step == 1:
        return index + 1 - 2 * lax.rem(index, 2)
    if step == 2:
        return index + 2 - 4 * lax.div(index, 2)
    return 3 - index


def combine(parts, coef):
    peak = functools.reduce(jnp.maximum, [m for _, m, _ in parts])
    total, weight = None, None
    for o, m, l in parts:
        factor = jnp.exp2((m - peak) * coef)
        o, l = o * factor, l * factor
        total = o if total is None else total + o
        weight = l if weight is None else weight + l
    return total, peak, weight


def stats(m, l):
    rows = lax.broadcasted_iota(jnp.int32, (8, m.shape[1]), 0)
    shape = (8, m.shape[1])
    return jnp.where(rows == 0, jnp.broadcast_to(m, shape), jnp.broadcast_to(l, shape))


def kernel(
    shards, kv_size, subs, rounds, piece,
    k_hbm, v_hbm, imp_hbm, asg_hbm, q_hbm,
    mk_ref, mv_ref, out_ref,
    k_ref, v_ref, imp_ref, asg_ref, q_ref, in_sems,
    kv_send, kv_recv, near_send, near_recv, far_send, far_recv, far_wide, arrived,
    num, q_t, k_ext, v_t,
    l1_send, l1_recv, s1_send, s1_recv, own_o, own_s,
    l2_send, l2_recv, s2_send, s2_recv,
    kv_ss, kv_rs, near_ss, near_rs, far_ss, far_rs,
    l1_ss, l1_rs, s1_ss, s1_rs, l2_ss, l2_rs, s2_ss, s2_rs,
    g2_ss, g2_rs, g1_ss, g1_rs,
):
    me = lax.axis_index("ctx")
    kv = lax.axis_index("kv")
    lo, hi = lax.rem(me, PLANE), lax.div(me, PLANE)
    high = shards // PLANE
    scatter = subs == high
    rows, width = k_ref.shape
    heads = width // LANES
    lanes = q_ref.shape[1]
    group_lanes = lanes // heads
    chunk = lanes // PLANE
    slots = 2 * NEAR + shards
    tiles = 2 * heads
    coef = math.log2(math.e) / math.sqrt(LANES)
    sent = []

    def put(src, dst, ss, rs, target):
        copy = pltpu.make_async_remote_copy(
            src_ref=src, dst_ref=dst, send_sem=ss, recv_sem=rs,
            device_id=target, device_id_type=MESH,
        )
        copy.start()
        sent.append(copy)
        return copy

    imp_in, asg_in, k_in, v_in, q_in = [
        pltpu.make_async_copy(src, dst, in_sems.at[n])
        for n, (src, dst) in enumerate((
            (imp_hbm, imp_ref), (asg_hbm, asg_ref), (k_hbm, k_ref), (v_hbm, v_ref),
            (q_hbm, q_ref),
        ))
    ]
    barrier = pltpu.get_barrier_semaphore()

    def greet(s, carry):
        pl.semaphore_signal(
            barrier, inc=1, device_id=(lax.rem(me + s, shards), kv), device_id_type=MESH
        )
        return carry

    for s in range(1, kv_size):
        pl.semaphore_signal(
            barrier, inc=1, device_id=(me, lax.rem(kv + s, kv_size)), device_id_type=MESH
        )
    lax.fori_loop(1, shards, greet, 0)
    for copy in (imp_in, asg_in, k_in, v_in, q_in):
        copy.start()

    imp_in.wait()
    part_weight = jnp.sum(imp_ref[...].astype(F32), axis=0, keepdims=True)
    kv_send[...] = jnp.broadcast_to(part_weight, (8, rows))
    for s in (0, 1, shards - 1):
        far_recv[s] = jnp.zeros((16, LANES), BF16)
    far_wide[...] = jnp.zeros_like(far_wide)

    asg_in.wait()
    asg = asg_ref[...]
    owner = jnp.right_shift(asg, rows.bit_length() - 1)
    target = jnp.bitwise_and(asg, rows - 1)
    distance = jnp.bitwise_and(owner - me, shards - 1)
    rank_row = lax.broadcasted_iota(jnp.int32, (16, rows), 0)
    distance_16 = jnp.broadcast_to(distance, (16, rows))
    wanted = jnp.where(rank_row == 0, 1, jnp.where(rank_row == 1, shards - 1, -1))
    marks = jnp.where(distance_16 == wanted, 1.0, 0.0).astype(BF16)
    earlier = jnp.where(
        lax.broadcasted_iota(jnp.int32, (rows, rows), 0)
        < lax.broadcasted_iota(jnp.int32, (rows, rows), 1),
        1.0, 0.0,
    ).astype(BF16)
    rank = dot(marks, earlier).astype(jnp.int32)
    key_next = jnp.where(distance == 1, rank[0:1], -1)
    key_prev = jnp.where(distance == shards - 1, rank[1:2], -1)
    far = jnp.where(distance >= 2, jnp.where(distance <= shards - 2, distance, -1), -1)

    def select(key, count):
        index = lax.broadcasted_iota(jnp.int32, (count, rows), 0)
        return jnp.where(jnp.broadcast_to(key, (count, rows)) == index, 1.0, 0.0)

    chosen = jnp.concatenate(
        [select(key_next, NEAR), select(key_prev, NEAR), select(far, shards)], axis=0
    )
    pl.semaphore_wait(barrier, shards - 1 + kv_size - 1)
    kv_copies = [
        put(kv_send, kv_recv.at[s], kv_ss.at[s], kv_rs.at[s], (me, lax.rem(kv + s, kv_size)))
        for s in range(1, kv_size)
    ]

    chosen_b = chosen.astype(BF16)
    k_in.wait()
    v_in.wait()
    out_rows = [dot(chosen_b, k_ref[...]), dot(chosen_b, v_ref[...])]
    meta_high = jnp.sum(
        chosen * jnp.right_shift(target, 7).astype(F32), axis=1, keepdims=True
    )
    meta_low = jnp.sum(
        chosen * jnp.bitwise_and(target, LANES - 1).astype(F32), axis=1, keepdims=True
    )
    for d in range(2):
        for part in range(2):
            near_send[d, :, part * width:(part + 1) * width] = out_rows[part][
                d * NEAR:(d + 1) * NEAR
            ].astype(BF16)
    for c in range(tiles):
        part, at = divmod(c, heads)
        far_wide[:, c, :] = out_rows[part][2 * NEAR:, at * LANES:(at + 1) * LANES]

    total_weight = part_weight
    for s, copy in enumerate(kv_copies, 1):
        copy.wait_recv()
        total_weight = total_weight + kv_recv[s, 0:1, :]
    weight = total_weight.astype(BF16).astype(F32)
    meta_weight = jnp.sum(chosen * weight, axis=1, keepdims=True)
    for m, meta in enumerate((meta_weight, meta_high, meta_low)):
        spread = jnp.broadcast_to(meta, (slots, LANES))
        for d in range(2):
            near_send[d, :, 2 * width + m * LANES:2 * width + (m + 1) * LANES] = spread[
                d * NEAR:(d + 1) * NEAR
            ].astype(BF16)
        far_wide[:, tiles + m, :] = spread[2 * NEAR:]
    far_send[...] = far_wide[...].astype(BF16)

    near_copies = [
        put(near_send.at[d], near_recv.at[d], near_ss.at[d], near_rs.at[d],
            (lax.rem(me + step, shards), kv))
        for d, step in enumerate((1, shards - 1))
    ]

    def far_copy(s):
        return pltpu.make_async_remote_copy(
            src_ref=far_send.at[s], dst_ref=far_recv.at[s],
            send_sem=far_ss.at[s], recv_sem=far_rs.at[s],
            device_id=(lax.rem(me + s, shards), kv), device_id_type=MESH,
        )

    def far_start(s, carry):
        far_copy(s).start()
        return carry

    def far_wait(s, carry):
        far_copy(s).wait()
        return carry

    lax.fori_loop(2, shards - 1, far_start, 0)

    home = jnp.where(distance == 0, target, -1)
    home_matrix = jnp.where(
        jnp.broadcast_to(home, (rows, rows))
        == lax.broadcasted_iota(jnp.int32, (rows, rows), 0),
        jnp.broadcast_to(weight, (rows, rows)), 0.0,
    ).astype(BF16)
    num[:, 0:width] = dot(home_matrix, k_ref[...])
    num[:, width:2 * width] = dot(home_matrix, v_ref[...])
    num[:, 2 * width:] = dot(home_matrix, jnp.ones((rows, LANES), BF16))
    q_in.wait()

    def turn_queries(j, carry):
        at = pl.ds(pl.multiple_of(j * 4 * LANES, 4 * LANES), 4 * LANES)
        group = q_ref[:, at]
        q_t[0:LANES, at] = jnp.concatenate(
            [group[:, n * LANES:(n + 1) * LANES].T for n in range(4)], axis=1
        )
        return carry

    lax.fori_loop(0, lanes // (4 * LANES), turn_queries, 0)
    q_t[LANES:, :] = jnp.ones((LANES, lanes), BF16)

    for copy in near_copies:
        copy.wait_recv()
    lax.fori_loop(2, shards - 1, far_wait, 0)

    far_wide[...] = far_recv[...].astype(F32)
    for d in range(2):
        arrived[d * NEAR:(d + 1) * NEAR, 0:2 * width] = near_recv[d, :, 0:2 * width]
    for c in range(tiles):
        arrived[2 * NEAR:, c * LANES:(c + 1) * LANES] = far_wide[:, c, :].astype(BF16)
    arrived[:, 2 * width:] = jnp.ones((slots, LANES), BF16)

    def meta_of(m):
        at = slice(2 * width + m * LANES, 2 * width + (m + 1) * LANES)
        return jnp.concatenate(
            [near_recv[0, :, at].astype(F32), near_recv[1, :, at].astype(F32),
             far_wide[:, tiles + m, :]], axis=0,
        )

    in_weight = meta_of(0)
    in_target = (meta_of(1) * LANES + meta_of(2)).astype(jnp.int32)
    lane = lax.broadcasted_iota(jnp.int32, (slots, LANES), 1)
    spread_t = jnp.concatenate(
        [jnp.where(in_target == lane + b * LANES, in_weight, 0.0) for b in range(rows // LANES)],
        axis=1,
    ).astype(BF16)

    num[...] += dot_t(spread_t, arrived[...])
    denominator = num[:, 2 * width:]
    kept = denominator > 0.0
    inverse = 1.0 / jnp.where(kept, denominator, 1.0)
    first_lane = lax.broadcasted_iota(jnp.int32, (rows, LANES), 1) == 0
    bias = jnp.where(first_lane, jnp.where(kept, 0.0, -1e30), 0.0).astype(BF16)
    for h in range(heads):
        at = slice(h * LANES, (h + 1) * LANES)
        far_at = slice(width + h * LANES, width + (h + 1) * LANES)
        key = num[:, at] * inverse
        key = jnp.where(kept, key, k_ref[:, at].astype(F32)).astype(BF16)
        mk_ref[:, at] = key
        k_ext[h, :, 0:LANES] = key
        k_ext[h, :, LANES:] = bias
        value = num[:, far_at] * inverse
        value = jnp.where(kept, value, v_ref[:, at].astype(F32)).astype(BF16)
        mv_ref[:, at] = value
        v_t[h, 0:LANES, :] = value.T
        v_t[h, LANES:, :] = jnp.ones((16, rows), BF16)

    def attend(column):
        h = lax.div(column, group_lanes)
        queries = q_t[:, pl.ds(pl.multiple_of(column, LANES), piece)]
        score = dot(k_ext[h], queries)
        peak = jnp.max(score, axis=0, keepdims=True)
        prob = jnp.exp2((score - peak) * coef).astype(BF16)
        both = dot(v_t[h], prob)
        return both[0:LANES], peak, both[LANES:LANES + 1]

    def sub_of(u):
        return lax.rem(hi + u, high) if scatter else 0

    wide = rounds * piece

    def place(part, sub, r):
        return part * chunk + sub * wide + r * piece

    def line(s):
        return (lax.rem(hi + s, high) * PLANE + lo, kv)

    across = {p: (hi * PLANE + flip(lo, p), kv) for p in (1, 2, 3)}
    l1_copies = {}

    def work(r, u):
        t = r * subs + u
        for s in (3, 1, 2, 0):
            dest = flip(lo, s) if s else lo
            o, m, l = attend(place(dest, sub_of(u), r))
            if s == 0:
                own_o[t] = o
                own_s[t] = stats(m, l)
                continue
            l1_send[s, t] = o.astype(BF16)
            s1_send[s, t] = stats(m, l)
            l1_copies[s, t] = (
                put(s1_send.at[s, t], s1_recv.at[s, t], s1_ss.at[s, t], s1_rs.at[s, t], across[s]),
                put(l1_send.at[s, t], l1_recv.at[s, t], l1_ss.at[s, t], l1_rs.at[s, t], across[s]),
            )

    def gather_plane(r, u):
        t = r * subs + u
        parts = [(own_o[t], own_s[t, 0:1, :], own_s[t, 1:2, :])]
        for s in (1, 2, 3):
            for copy in l1_copies[s, t]:
                copy.wait_recv()
            parts.append(
                (l1_recv[s, t].astype(F32), s1_recv[s, t, 0:1, :], s1_recv[s, t, 1:2, :])
            )
        return combine(parts, coef)

    l2_copies = []

    def forward(r, u):
        o, m, l = gather_plane(r, u)
        t = r * high + u
        l2_send[t] = o.astype(BF16)
        s2_send[t] = stats(m, l)
        l2_copies.append((
            r, t,
            put(s2_send.at[t], s2_recv.at[t], s2_ss.at[t], s2_rs.at[t], line(u)),
            put(l2_send.at[t], l2_recv.at[t], l2_ss.at[t], l2_rs.at[t], line(u)),
        ))

    def gather_line(r):
        o, m, l = gather_plane(r, 0)
        base = r * high
        if scatter:
            parts = [(o, m, l)]
            for n, t, first, second in l2_copies:
                if n == r:
                    first.wait_recv()
                    second.wait_recv()
                    parts.append((l2_recv[t].astype(F32), s2_recv[t, 0:1, :], s2_recv[t, 1:2, :]))
        else:
            l2_send[base] = o.astype(BF16)
            s2_send[base] = stats(m, l)
            l2_recv[base + hi] = o.astype(BF16)
            s2_recv[base + hi] = stats(m, l)
            for s in range(1, high):
                put(s2_send.at[base], s2_recv.at[base + hi], s2_ss.at[base + s],
                    s2_rs.at[base + hi], line(s))
                put(l2_send.at[base], l2_recv.at[base + hi], l2_ss.at[base + s],
                    l2_rs.at[base + hi], line(s))
            for s in range(1, high):
                other = base + lax.rem(hi + s, high)
                for src, dst, ss, rs in (
                    (s2_send, s2_recv, s2_ss, s2_rs), (l2_send, l2_recv, l2_ss, l2_rs),
                ):
                    pltpu.make_async_remote_copy(
                        src_ref=src.at[base], dst_ref=dst.at[other], send_sem=ss.at[base + s],
                        recv_sem=rs.at[other], device_id=line(s), device_id_type=MESH,
                    ).wait_recv()
            parts = [
                (l2_recv[base + j].astype(F32), s2_recv[base + j, 0:1, :],
                 s2_recv[base + j, 1:2, :])
                for j in range(high)
            ]
        return combine(parts, coef)

    def block(column):
        return out_ref.at[:, pl.ds(pl.multiple_of(column, LANES), piece)]

    def from_line(r, s, p=0):
        part = flip(lo, p) if p else lo
        return place(part, lax.rem(hi - s + high, high) if scatter else 0, r)

    def await_copy(view, ss, rs):
        pltpu.make_async_remote_copy(
            src_ref=view, dst_ref=view, send_sem=ss, recv_sem=rs,
            device_id=line(1), device_id_type=MESH,
        ).wait_recv()

    def to_plane(r, s):
        view, t = block(from_line(r, s)), r * subs + s
        for p in (1, 2):
            put(view, view, g1_ss.at[p, t], g1_rs.at[p, t], across[p])

    def finish(r):
        o, _, l = gather_line(r)
        result = o * (1.0 / l)
        mine = from_line(r, 0)
        for j in range(piece // LANES):
            at = pl.ds(pl.multiple_of(mine + j * LANES, LANES), LANES)
            out_ref[:, at] = result[:, j * LANES:(j + 1) * LANES].T.astype(BF16)
        if scatter:
            for s in range(1, high):
                t = r * high + s
                put(block(mine), block(mine), g2_ss.at[t], g2_rs.at[t], line(s))
        to_plane(r, 0)

    def spread_line(r, s):
        t = r * high + s
        await_copy(block(from_line(r, s)), g2_ss.at[t], g2_rs.at[t])
        to_plane(r, s)

    def pass_on(r, s):
        p = 1 + (r + s) % 2
        t = r * subs + s
        view = block(from_line(r, s, p))
        await_copy(view, g1_ss.at[p, t], g1_rs.at[p, t])
        put(view, view, g1_ss.at[3, t], g1_rs.at[3, t], across[3 - p])

    def last_waits(r, s):
        t = r * subs + s
        for p in (2 - (r + s) % 2, 3):
            await_copy(block(from_line(r, s, p)), g1_ss.at[p, t], g1_rs.at[p, t])

    order = list(range(1, subs)) + [0]
    pending = []
    for r in range(rounds):
        for n, u in enumerate(order):
            work(r, u)
            if n >= 1:
                forward(r, order[n - 1])
            for step in pending[n::subs]:
                step()
        if r < rounds - 1:
            pending = [functools.partial(finish, r)]
            pending += [functools.partial(spread_line, r, s) for s in range(1, subs)]
    finish(rounds - 1)
    for s in range(subs):
        for r in range(rounds - 1):
            pass_on(r, s)
    for s in range(1, subs):
        spread_line(rounds - 1, s)
        pass_on(rounds - 1, s - 1)
    pass_on(rounds - 1, subs - 1)
    for r in range(rounds):
        for s in range(subs):
            last_waits(r, s)
    for copy in sent:
        copy.wait_send()


def per_device(cache_keys, cache_values, importance, assignment, queries):
    shards = lax.axis_size("ctx")
    kv_size = lax.axis_size("kv")
    rows, width = cache_keys.shape
    lanes = queries.shape[1]
    high = shards // PLANE
    subs = high if (lanes // PLANE) % (high * LANES) == 0 else 1
    rounds = 2 if (lanes // PLANE // subs) % (2 * LANES) == 0 else 1
    piece = lanes // PLANE // subs // rounds
    steps = rounds * subs
    heads = width // LANES
    slots = 2 * NEAR + shards
    wide = 2 * width + 3 * LANES
    dma = pltpu.SemaphoreType.DMA
    vmem = pl.BlockSpec(memory_space=pltpu.VMEM)
    hbm = pl.BlockSpec(memory_space=pltpu.HBM)
    body = functools.partial(kernel, shards, kv_size, subs, rounds, piece)
    shapes = (
        jax.ShapeDtypeStruct((rows, width), BF16),
        jax.ShapeDtypeStruct((rows, width), BF16),
        jax.ShapeDtypeStruct(queries.shape, BF16),
    )
    call = pl.pallas_call(
        body,
        out_shape=tuple(pltpu.VMEM(x.shape, x.dtype) for x in shapes),
        in_specs=[hbm] * 5,
        out_specs=(vmem,) * 3,
        scratch_shapes=[
            pltpu.VMEM((rows, width), BF16),
            pltpu.VMEM((rows, width), BF16),
            pltpu.VMEM(importance.shape, BF16),
            pltpu.VMEM((1, rows), jnp.int32),
            pltpu.VMEM(queries.shape, BF16),
            dma((5,)),
            pltpu.VMEM((8, rows), F32),
            pltpu.VMEM((kv_size, 8, rows), F32),
            pltpu.VMEM((2, NEAR, wide), BF16),
            pltpu.VMEM((2, NEAR, wide), BF16),
            pltpu.VMEM((shards, 16, LANES), BF16),
            pltpu.VMEM((shards, 16, LANES), BF16),
            pltpu.VMEM((shards, 16, LANES), F32),
            pltpu.VMEM((slots, 2 * width + LANES), BF16),
            pltpu.VMEM((rows, 2 * width + LANES), F32),
            pltpu.VMEM((2 * LANES, lanes), BF16),
            pltpu.VMEM((heads, rows, 2 * LANES), BF16),
            pltpu.VMEM((heads, LANES + 16, rows), BF16),
            pltpu.VMEM((PLANE, steps, LANES, piece), BF16),
            pltpu.VMEM((PLANE, steps, LANES, piece), BF16),
            pltpu.VMEM((PLANE, steps, 8, piece), F32),
            pltpu.VMEM((PLANE, steps, 8, piece), F32),
            pltpu.VMEM((steps, LANES, piece), F32),
            pltpu.VMEM((steps, 8, piece), F32),
            pltpu.VMEM((rounds * high, LANES, piece), BF16),
            pltpu.VMEM((rounds * high, LANES, piece), BF16),
            pltpu.VMEM((rounds * high, 8, piece), F32),
            pltpu.VMEM((rounds * high, 8, piece), F32),
            dma((kv_size,)), dma((kv_size,)),
            dma((2,)), dma((2,)),
            dma((shards,)), dma((shards,)),
            dma((PLANE, steps)), dma((PLANE, steps)),
            dma((PLANE, steps)), dma((PLANE, steps)),
            dma((rounds * high,)), dma((rounds * high,)),
            dma((rounds * high,)), dma((rounds * high,)),
            dma((rounds * high,)), dma((rounds * high,)),
            dma((PLANE, steps)), dma((PLANE, steps)),
        ],
        compiler_params=pltpu.CompilerParams(
            collective_id=0, has_side_effects=True, vmem_limit_bytes=40 * 1024 * 1024
        ),
    )
    operands = (cache_keys, cache_values, importance, assignment.reshape(1, rows), queries)
    return call(*(pltpu.with_memory_space_constraint(x, pltpu.HBM) for x in operands))


def solution(mesh):
    placed = (P("ctx", "kv"), P("ctx", "kv"), P("kv", "ctx"), P("ctx"), P(None, "kv"))
    return jax.shard_map(
        per_device,
        mesh=mesh,
        in_specs=placed,
        out_specs=(P("ctx", "kv"), P("ctx", "kv"), P(None, "kv")),
        check_vma=False,
    )
```

```python
import functools
import math

import jax
import jax.numpy as jnp
from jax import lax
from jax.experimental import pallas as pl
from jax.experimental.pallas import tpu as pltpu
from jax.sharding import PartitionSpec as P

NEAR = 16
LANES = 128
PLANE = 4
MESH = pl.DeviceIdType.MESH
F32 = jnp.float32
BF16 = jnp.bfloat16


def dot(a, b):
    return jnp.dot(a, b, preferred_element_type=F32)


def dot_t(a, b):
    return lax.dot_general(a, b, (((0,), (0,)), ((), ())), preferred_element_type=F32)


def flip(index, step):
    if step == 1:
        return index + 1 - 2 * lax.rem(index, 2)
    if step == 2:
        return index + 2 - 4 * lax.div(index, 2)
    return 3 - index


def combine(parts, coef):
    peak = functools.reduce(jnp.maximum, [m for _, m, _ in parts])
    total, weight = None, None
    for o, m, l in parts:
        factor = jnp.exp2((m - peak) * coef)
        o, l = o * factor, l * factor
        total = o if total is None else total + o
        weight = l if weight is None else weight + l
    return total, peak, weight


def stats(m, l):
    rows = lax.broadcasted_iota(jnp.int32, (8, m.shape[1]), 0)
    shape = (8, m.shape[1])
    return jnp.where(rows == 0, jnp.broadcast_to(m, shape), jnp.broadcast_to(l, shape))


def kernel(
    shards, kv_size, subs, rounds, piece,
    k_hbm, v_hbm, imp_hbm, asg_hbm, q_hbm,
    mk_ref, mv_ref, out_ref,
    k_ref, v_ref, imp_ref, asg_ref, q_ref, in_sems,
    kv_send, kv_recv, near_send, near_recv, far_send, far_recv, far_wide, arrived,
    num, q_t, k_ext, v_t,
    l1_send, l1_recv, s1_send, s1_recv, own_o, own_s,
    l2_send, l2_recv, s2_send, s2_recv,
    kv_ss, kv_rs, near_ss, near_rs, far_ss, far_rs,
    l1_ss, l1_rs, s1_ss, s1_rs, l2_ss, l2_rs, s2_ss, s2_rs,
    g2_ss, g2_rs, g1_ss, g1_rs,
):
    me = lax.axis_index("ctx")
    kv = lax.axis_index("kv")
    lo, hi = lax.rem(me, PLANE), lax.div(me, PLANE)
    high = shards // PLANE
    scatter = subs == high
    rows, width = k_ref.shape
    heads = width // LANES
    lanes = q_ref.shape[1]
    group_lanes = lanes // heads
    chunk = lanes // PLANE
    slots = 2 * NEAR + shards
    tiles = 2 * heads
    coef = math.log2(math.e) / math.sqrt(LANES)
    sent = []

    def put(src, dst, ss, rs, target):
        copy = pltpu.make_async_remote_copy(
            src_ref=src, dst_ref=dst, send_sem=ss, recv_sem=rs,
            device_id=target, device_id_type=MESH,
        )
        copy.start()
        sent.append(copy)
        return copy

    imp_in, asg_in, k_in, v_in, q_in = [
        pltpu.make_async_copy(src, dst, in_sems.at[n])
        for n, (src, dst) in enumerate((
            (imp_hbm, imp_ref), (asg_hbm, asg_ref), (k_hbm, k_ref), (v_hbm, v_ref),
            (q_hbm, q_ref),
        ))
    ]
    barrier = pltpu.get_barrier_semaphore()

    def greet(s, carry):
        pl.semaphore_signal(
            barrier, inc=1, device_id=(lax.rem(me + s, shards), kv), device_id_type=MESH
        )
        return carry

    for s in range(1, kv_size):
        pl.semaphore_signal(
            barrier, inc=1, device_id=(me, lax.rem(kv + s, kv_size)), device_id_type=MESH
        )
    lax.fori_loop(1, shards, greet, 0)
    for copy in (imp_in, asg_in, k_in, v_in, q_in):
        copy.start()

    imp_in.wait()
    part_weight = jnp.sum(imp_ref[...].astype(F32), axis=0, keepdims=True)
    kv_send[...] = jnp.broadcast_to(part_weight, (8, rows))
    for s in (0, 1, shards - 1):
        far_recv[s] = jnp.zeros((16, LANES), BF16)
    far_wide[...] = jnp.zeros_like(far_wide)

    asg_in.wait()
    asg = asg_ref[...]
    owner = jnp.right_shift(asg, rows.bit_length() - 1)
    target = jnp.bitwise_and(asg, rows - 1)
    distance = jnp.bitwise_and(owner - me, shards - 1)
    rank_row = lax.broadcasted_iota(jnp.int32, (16, rows), 0)
    distance_16 = jnp.broadcast_to(distance, (16, rows))
    wanted = jnp.where(rank_row == 0, 1, jnp.where(rank_row == 1, shards - 1, -1))
    marks = jnp.where(distance_16 == wanted, 1.0, 0.0).astype(BF16)
    earlier = jnp.where(
        lax.broadcasted_iota(jnp.int32, (rows, rows), 0)
        < lax.broadcasted_iota(jnp.int32, (rows, rows), 1),
        1.0, 0.0,
    ).astype(BF16)
    rank = dot(marks, earlier).astype(jnp.int32)
    key_next = jnp.where(distance == 1, rank[0:1], -1)
    key_prev = jnp.where(distance == shards - 1, rank[1:2], -1)
    far = jnp.where(distance >= 2, jnp.where(distance <= shards - 2, distance, -1), -1)

    def select(key, count):
        index = lax.broadcasted_iota(jnp.int32, (count, rows), 0)
        return jnp.where(jnp.broadcast_to(key, (count, rows)) == index, 1.0, 0.0)

    chosen = jnp.concatenate(
        [select(key_next, NEAR), select(key_prev, NEAR), select(far, shards)], axis=0
    )
    pl.semaphore_wait(barrier, shards - 1 + kv_size - 1)
    kv_copies = [
        put(kv_send, kv_recv.at[s], kv_ss.at[s], kv_rs.at[s], (me, lax.rem(kv + s, kv_size)))
        for s in range(1, kv_size)
    ]

    chosen_b = chosen.astype(BF16)
    k_in.wait()
    v_in.wait()
    out_rows = [dot(chosen_b, k_ref[...]), dot(chosen_b, v_ref[...])]
    meta_high = jnp.sum(
        chosen * jnp.right_shift(target, 7).astype(F32), axis=1, keepdims=True
    )
    meta_low = jnp.sum(
        chosen * jnp.bitwise_and(target, LANES - 1).astype(F32), axis=1, keepdims=True
    )
    for d in range(2):
        for part in range(2):
            near_send[d, :, part * width:(part + 1) * width] = out_rows[part][
                d * NEAR:(d + 1) * NEAR
            ].astype(BF16)
    for c in range(tiles):
        part, at = divmod(c, heads)
        far_wide[:, c, :] = out_rows[part][2 * NEAR:, at * LANES:(at + 1) * LANES]

    total_weight = part_weight
    for s, copy in enumerate(kv_copies, 1):
        copy.wait_recv()
        total_weight = total_weight + kv_recv[s, 0:1, :]
    weight = total_weight.astype(BF16).astype(F32)
    meta_weight = jnp.sum(chosen * weight, axis=1, keepdims=True)
    for m, meta in enumerate((meta_weight, meta_high, meta_low)):
        spread = jnp.broadcast_to(meta, (slots, LANES))
        for d in range(2):
            near_send[d, :, 2 * width + m * LANES:2 * width + (m + 1) * LANES] = spread[
                d * NEAR:(d + 1) * NEAR
            ].astype(BF16)
        far_wide[:, tiles + m, :] = spread[2 * NEAR:]
    far_send[...] = far_wide[...].astype(BF16)

    near_copies = [
        put(near_send.at[d], near_recv.at[d], near_ss.at[d], near_rs.at[d],
            (lax.rem(me + step, shards), kv))
        for d, step in enumerate((1, shards - 1))
    ]

    def far_copy(s):
        return pltpu.make_async_remote_copy(
            src_ref=far_send.at[s], dst_ref=far_recv.at[s],
            send_sem=far_ss.at[s], recv_sem=far_rs.at[s],
            device_id=(lax.rem(me + s, shards), kv), device_id_type=MESH,
        )

    def far_start(s, carry):
        far_copy(s).start()
        return carry

    def far_wait(s, carry):
        far_copy(s).wait()
        return carry

    lax.fori_loop(2, shards - 1, far_start, 0)

    home = jnp.where(distance == 0, target, -1)
    home_matrix = jnp.where(
        jnp.broadcast_to(home, (rows, rows))
        == lax.broadcasted_iota(jnp.int32, (rows, rows), 0),
        jnp.broadcast_to(weight, (rows, rows)), 0.0,
    ).astype(BF16)
    num[:, 0:width] = dot(home_matrix, k_ref[...])
    num[:, width:2 * width] = dot(home_matrix, v_ref[...])
    num[:, 2 * width:] = dot(home_matrix, jnp.ones((rows, LANES), BF16))
    q_in.wait()

    def turn_queries(j, carry):
        at = pl.ds(pl.multiple_of(j * 4 * LANES, 4 * LANES), 4 * LANES)
        group = q_ref[:, at]
        q_t[0:LANES, at] = jnp.concatenate(
            [group[:, n * LANES:(n + 1) * LANES].T for n in range(4)], axis=1
        )
        return carry

    lax.fori_loop(0, lanes // (4 * LANES), turn_queries, 0)
    q_t[LANES:, :] = jnp.ones((LANES, lanes), BF16)

    for copy in near_copies:
        copy.wait_recv()
    lax.fori_loop(2, shards - 1, far_wait, 0)

    far_wide[...] = far_recv[...].astype(F32)
    for d in range(2):
        arrived[d * NEAR:(d + 1) * NEAR, 0:2 * width] = near_recv[d, :, 0:2 * width]
    for c in range(tiles):
        arrived[2 * NEAR:, c * LANES:(c + 1) * LANES] = far_wide[:, c, :].astype(BF16)
    arrived[:, 2 * width:] = jnp.ones((slots, LANES), BF16)

    def meta_of(m):
        at = slice(2 * width + m * LANES, 2 * width + (m + 1) * LANES)
        return jnp.concatenate(
            [near_recv[0, :, at].astype(F32), near_recv[1, :, at].astype(F32),
             far_wide[:, tiles + m, :]], axis=0,
        )

    in_weight = meta_of(0)
    in_target = (meta_of(1) * LANES + meta_of(2)).astype(jnp.int32)
    lane = lax.broadcasted_iota(jnp.int32, (slots, LANES), 1)
    spread_t = jnp.concatenate(
        [jnp.where(in_target == lane + b * LANES, in_weight, 0.0) for b in range(rows // LANES)],
        axis=1,
    ).astype(BF16)

    num[...] += dot_t(spread_t, arrived[...])
    denominator = num[:, 2 * width:]
    kept = denominator > 0.0
    inverse = 1.0 / jnp.where(kept, denominator, 1.0)
    first_lane = lax.broadcasted_iota(jnp.int32, (rows, LANES), 1) == 0
    bias = jnp.where(first_lane, jnp.where(kept, 0.0, -1e30), 0.0).astype(BF16)
    for h in range(heads):
        at = slice(h * LANES, (h + 1) * LANES)
        far_at = slice(width + h * LANES, width + (h + 1) * LANES)
        key = num[:, at] * inverse
        key = jnp.where(kept, key, k_ref[:, at].astype(F32)).astype(BF16)
        mk_ref[:, at] = key
        k_ext[h, :, 0:LANES] = key
        k_ext[h, :, LANES:] = bias
        value = num[:, far_at] * inverse
        value = jnp.where(kept, value, v_ref[:, at].astype(F32)).astype(BF16)
        mv_ref[:, at] = value
        v_t[h, 0:LANES, :] = value.T
        v_t[h, LANES:, :] = jnp.ones((16, rows), BF16)

    def attend(columns):
        def score_of(column):
            queries = q_t[:, pl.ds(pl.multiple_of(column, LANES), piece)]
            return dot(k_ext[lax.div(column, group_lanes)], queries)

        results = []
        score = score_of(columns[0])
        for n, column in enumerate(columns):
            ahead = score_of(columns[n + 1]) if n + 1 < len(columns) else None
            peak = jnp.max(score, axis=0, keepdims=True)
            prob = jnp.exp2((score - peak) * coef).astype(BF16)
            both = dot(v_t[lax.div(column, group_lanes)], prob)
            results.append((both[0:LANES], peak, both[LANES:LANES + 1]))
            score = ahead
        return results

    def sub_of(u):
        return lax.rem(hi + u, high) if scatter else 0

    wide = rounds * piece

    def place(part, sub, r):
        return part * chunk + sub * wide + r * piece

    def line(s):
        return (lax.rem(hi + s, high) * PLANE + lo, kv)

    across = {p: (hi * PLANE + flip(lo, p), kv) for p in (1, 2, 3)}

    def hop(s, t):
        return [
            pltpu.make_async_remote_copy(
                src_ref=src.at[s, t], dst_ref=dst.at[s, t], send_sem=ss.at[s, t],
                recv_sem=rs.at[s, t], device_id=across[s], device_id_type=MESH,
            )
            for src, dst, ss, rs in (
                (s1_send, s1_recv, s1_ss, s1_rs), (l1_send, l1_recv, l1_ss, l1_rs),
            )
        ]

    def hop_line(t):
        return [
            pltpu.make_async_remote_copy(
                src_ref=src.at[t], dst_ref=dst.at[t], send_sem=ss.at[t],
                recv_sem=rs.at[t], device_id=line(t), device_id_type=MESH,
            )
            for src, dst, ss, rs in (
                (s2_send, s2_recv, s2_ss, s2_rs), (l2_send, l2_recv, l2_ss, l2_rs),
            )
        ]

    def work(t):
        steps = (3, 1, 2, 0)
        places = [place(flip(lo, s) if s else lo, sub_of(t), 0) for s in steps]
        for s, (o, m, l) in zip(steps, attend(places)):
            if s == 0:
                own_o[t] = o
                own_s[t] = stats(m, l)
            else:
                l1_send[s, t] = o.astype(BF16)
                s1_send[s, t] = stats(m, l)
        for s in (3, 1, 2):
            for copy in hop(s, t):
                copy.start()

    def gather_plane(t):
        parts = [(own_o[t], own_s[t, 0:1, :], own_s[t, 1:2, :])]
        for s in (1, 2, 3):
            for copy in hop(s, t):
                copy.wait_recv()
            parts.append(
                (l1_recv[s, t].astype(F32), s1_recv[s, t, 0:1, :], s1_recv[s, t, 1:2, :])
            )
        return combine(parts, coef)

    def forward(t):
        o, m, l = gather_plane(t)
        l2_send[t] = o.astype(BF16)
        s2_send[t] = stats(m, l)
        for copy in hop_line(t):
            copy.start()

    def turn(n, carry):
        work(lax.rem(n + 1, subs))

        @pl.when(n >= 1)
        def _():
            forward(n)

        return carry

    def gather_line(r):
        o, m, l = gather_plane(0)
        base = r * high
        if scatter:
            parts = [(o, m, l)]
            for t in range(1, high):
                for copy in hop_line(t):
                    copy.wait_recv()
                parts.append((l2_recv[t].astype(F32), s2_recv[t, 0:1, :], s2_recv[t, 1:2, :]))
        else:
            l2_send[base] = o.astype(BF16)
            s2_send[base] = stats(m, l)
            l2_recv[base + hi] = o.astype(BF16)
            s2_recv[base + hi] = stats(m, l)
            for s in range(1, high):
                put(s2_send.at[base], s2_recv.at[base + hi], s2_ss.at[base + s],
                    s2_rs.at[base + hi], line(s))
                put(l2_send.at[base], l2_recv.at[base + hi], l2_ss.at[base + s],
                    l2_rs.at[base + hi], line(s))
            for s in range(1, high):
                other = base + lax.rem(hi + s, high)
                for src, dst, ss, rs in (
                    (s2_send, s2_recv, s2_ss, s2_rs), (l2_send, l2_recv, l2_ss, l2_rs),
                ):
                    pltpu.make_async_remote_copy(
                        src_ref=src.at[base], dst_ref=dst.at[other], send_sem=ss.at[base + s],
                        recv_sem=rs.at[other], device_id=line(s), device_id_type=MESH,
                    ).wait_recv()
            parts = [
                (l2_recv[base + j].astype(F32), s2_recv[base + j, 0:1, :],
                 s2_recv[base + j, 1:2, :])
                for j in range(high)
            ]
        return combine(parts, coef)

    def block(column):
        return out_ref.at[:, pl.ds(pl.multiple_of(column, LANES), piece)]

    def from_line(r, s, p=0):
        part = flip(lo, p) if p else lo
        return place(part, lax.rem(hi - s + high, high) if scatter else 0, r)

    def await_copy(view, ss, rs):
        pltpu.make_async_remote_copy(
            src_ref=view, dst_ref=view, send_sem=ss, recv_sem=rs,
            device_id=line(1), device_id_type=MESH,
        ).wait_recv()

    def to_plane(r, s):
        view, t = block(from_line(r, s)), r * subs + s
        for p in (1, 2):
            put(view, view, g1_ss.at[p, t], g1_rs.at[p, t], across[p])

    def finish(r):
        o, _, l = gather_line(r)
        result = o * (1.0 / l)
        mine = from_line(r, 0)
        for j in range(piece // LANES):
            at = pl.ds(pl.multiple_of(mine + j * LANES, LANES), LANES)
            out_ref[:, at] = result[:, j * LANES:(j + 1) * LANES].T.astype(BF16)
        if scatter:
            for s in range(1, high):
                t = r * high + s
                put(block(mine), block(mine), g2_ss.at[t], g2_rs.at[t], line(s))
        to_plane(r, 0)

    def spread_line(r, s):
        t = r * high + s
        await_copy(block(from_line(r, s)), g2_ss.at[t], g2_rs.at[t])
        to_plane(r, s)

    def pass_on(r, s):
        p = 1 + (r + s) % 2
        t = r * subs + s
        view = block(from_line(r, s, p))
        await_copy(view, g1_ss.at[p, t], g1_rs.at[p, t])
        put(view, view, g1_ss.at[3, t], g1_rs.at[3, t], across[3 - p])

    def last_waits(r, s):
        t = r * subs + s
        for p in (2 - (r + s) % 2, 3):
            await_copy(block(from_line(r, s, p)), g1_ss.at[p, t], g1_rs.at[p, t])

    lax.fori_loop(0, subs, turn, 0)
    finish(rounds - 1)
    for s in range(subs):
        for r in range(rounds - 1):
            pass_on(r, s)
    for s in range(1, subs):
        spread_line(rounds - 1, s)
        pass_on(rounds - 1, s - 1)
    pass_on(rounds - 1, subs - 1)
    for r in range(rounds):
        for s in range(subs):
            last_waits(r, s)
    for copy in sent:
        copy.wait_send()

    def drain(t, carry):
        for s in (1, 2, 3):
            for copy in hop(s, t):
                copy.wait_send()
        if scatter:
            @pl.when(t >= 1)
            def _():
                for copy in hop_line(t):
                    copy.wait_send()
        return carry

    lax.fori_loop(0, subs, drain, 0)


def per_device(cache_keys, cache_values, importance, assignment, queries):
    shards = lax.axis_size("ctx")
    kv_size = lax.axis_size("kv")
    rows, width = cache_keys.shape
    lanes = queries.shape[1]
    high = shards // PLANE
    subs = high if (lanes // PLANE) % (high * LANES) == 0 else 1
    rounds = 1
    piece = lanes // PLANE // subs // rounds
    steps = rounds * subs
    heads = width // LANES
    slots = 2 * NEAR + shards
    wide = 2 * width + 3 * LANES
    dma = pltpu.SemaphoreType.DMA
    vmem = pl.BlockSpec(memory_space=pltpu.VMEM)
    hbm = pl.BlockSpec(memory_space=pltpu.HBM)
    body = functools.partial(kernel, shards, kv_size, subs, rounds, piece)
    shapes = (
        jax.ShapeDtypeStruct((rows, width), BF16),
        jax.ShapeDtypeStruct((rows, width), BF16),
        jax.ShapeDtypeStruct(queries.shape, BF16),
    )
    call = pl.pallas_call(
        body,
        out_shape=tuple(pltpu.VMEM(x.shape, x.dtype) for x in shapes),
        in_specs=[hbm] * 5,
        out_specs=(vmem,) * 3,
        scratch_shapes=[
            pltpu.VMEM((rows, width), BF16),
            pltpu.VMEM((rows, width), BF16),
            pltpu.VMEM(importance.shape, BF16),
            pltpu.VMEM((1, rows), jnp.int32),
            pltpu.VMEM(queries.shape, BF16),
            dma((5,)),
            pltpu.VMEM((8, rows), F32),
            pltpu.VMEM((kv_size, 8, rows), F32),
            pltpu.VMEM((2, NEAR, wide), BF16),
            pltpu.VMEM((2, NEAR, wide), BF16),
            pltpu.VMEM((shards, 16, LANES), BF16),
            pltpu.VMEM((shards, 16, LANES), BF16),
            pltpu.VMEM((shards, 16, LANES), F32),
            pltpu.VMEM((slots, 2 * width + LANES), BF16),
            pltpu.VMEM((rows, 2 * width + LANES), F32),
            pltpu.VMEM((2 * LANES, lanes), BF16),
            pltpu.VMEM((heads, rows, 2 * LANES), BF16),
            pltpu.VMEM((heads, LANES + 16, rows), BF16),
            pltpu.VMEM((PLANE, steps, LANES, piece), BF16),
            pltpu.VMEM((PLANE, steps, LANES, piece), BF16),
            pltpu.VMEM((PLANE, steps, 8, piece), F32),
            pltpu.VMEM((PLANE, steps, 8, piece), F32),
            pltpu.VMEM((steps, LANES, piece), F32),
            pltpu.VMEM((steps, 8, piece), F32),
            pltpu.VMEM((rounds * high, LANES, piece), BF16),
            pltpu.VMEM((rounds * high, LANES, piece), BF16),
            pltpu.VMEM((rounds * high, 8, piece), F32),
            pltpu.VMEM((rounds * high, 8, piece), F32),
            dma((kv_size,)), dma((kv_size,)),
            dma((2,)), dma((2,)),
            dma((shards,)), dma((shards,)),
            dma((PLANE, steps)), dma((PLANE, steps)),
            dma((PLANE, steps)), dma((PLANE, steps)),
            dma((rounds * high,)), dma((rounds * high,)),
            dma((rounds * high,)), dma((rounds * high,)),
            dma((rounds * high,)), dma((rounds * high,)),
            dma((PLANE, steps)), dma((PLANE, steps)),
        ],
        compiler_params=pltpu.CompilerParams(
            collective_id=0, has_side_effects=True, vmem_limit_bytes=40 * 1024 * 1024
        ),
    )
    operands = (cache_keys, cache_values, importance, assignment.reshape(1, rows), queries)
    return call(*(pltpu.with_memory_space_constraint(x, pltpu.HBM) for x in operands))


def solution(mesh):
    placed = (P("ctx", "kv"), P("ctx", "kv"), P("kv", "ctx"), P("ctx"), P(None, "kv"))
    return jax.shard_map(
        per_device,
        mesh=mesh,
        in_specs=placed,
        out_specs=(P("ctx", "kv"), P("ctx", "kv"), P(None, "kv")),
        check_vma=False,
    )
```

```python
import functools
import math

import jax
import jax.numpy as jnp
from jax import lax
from jax.experimental import pallas as pl
from jax.experimental.pallas import tpu as pltpu
from jax.sharding import PartitionSpec as P

NEAR = 16
LANES = 128
PLANE = 4
MESH = pl.DeviceIdType.MESH
F32 = jnp.float32
BF16 = jnp.bfloat16


def dot(a, b):
    return jnp.dot(a, b, preferred_element_type=F32)


def dot_t(a, b):
    return lax.dot_general(a, b, (((0,), (0,)), ((), ())), preferred_element_type=F32)


def flip(index, step):
    if step == 1:
        return index + 1 - 2 * lax.rem(index, 2)
    if step == 2:
        return index + 2 - 4 * lax.div(index, 2)
    return 3 - index


def combine(parts, coef):
    peak = functools.reduce(jnp.maximum, [m for _, m, _ in parts])
    total, weight = None, None
    for o, m, l in parts:
        factor = jnp.exp2((m - peak) * coef)
        o, l = o * factor, l * factor
        total = o if total is None else total + o
        weight = l if weight is None else weight + l
    return total, peak, weight


def stats(m, l):
    rows = lax.broadcasted_iota(jnp.int32, (8, m.shape[1]), 0)
    shape = (8, m.shape[1])
    return jnp.where(rows == 0, jnp.broadcast_to(m, shape), jnp.broadcast_to(l, shape))


def kernel(
    shards, kv_size, subs, rounds, piece,
    k_hbm, v_hbm, imp_hbm, asg_hbm, q_hbm,
    mk_ref, mv_ref, out_ref,
    k_ref, v_ref, imp_ref, asg_ref, q_ref, in_sems,
    kv_send, kv_recv, near_send, near_recv, far_send, far_recv, far_wide, arrived,
    num, q_t, k_ext, v_t,
    l1_send, l1_recv, s1_send, s1_recv, own_o, own_s,
    l2_send, l2_recv, s2_send, s2_recv,
    kv_ss, kv_rs, near_ss, near_rs, far_ss, far_rs,
    l1_ss, l1_rs, s1_ss, s1_rs, l2_ss, l2_rs, s2_ss, s2_rs,
    g2_ss, g2_rs, g1_ss, g1_rs,
):
    me = lax.axis_index("ctx")
    kv = lax.axis_index("kv")
    lo, hi = lax.rem(me, PLANE), lax.div(me, PLANE)
    high = shards // PLANE
    scatter = subs == high
    rows, width = k_ref.shape
    heads = width // LANES
    lanes = q_ref.shape[1]
    group_lanes = lanes // heads
    chunk = lanes // PLANE
    slots = 2 * NEAR + shards
    tiles = 2 * heads
    coef = math.log2(math.e) / math.sqrt(LANES)
    sent = []

    def put(src, dst, ss, rs, target):
        copy = pltpu.make_async_remote_copy(
            src_ref=src, dst_ref=dst, send_sem=ss, recv_sem=rs,
            device_id=target, device_id_type=MESH,
        )
        copy.start()
        sent.append(copy)
        return copy

    imp_in, asg_in, k_in, v_in, q_in = [
        pltpu.make_async_copy(src, dst, in_sems.at[n])
        for n, (src, dst) in enumerate((
            (imp_hbm, imp_ref), (asg_hbm, asg_ref), (k_hbm, k_ref), (v_hbm, v_ref),
            (q_hbm, q_ref),
        ))
    ]
    barrier = pltpu.get_barrier_semaphore()

    def greet(s, carry):
        pl.semaphore_signal(
            barrier, inc=1, device_id=(lax.rem(me + s, shards), kv), device_id_type=MESH
        )
        return carry

    for s in range(1, kv_size):
        pl.semaphore_signal(
            barrier, inc=1, device_id=(me, lax.rem(kv + s, kv_size)), device_id_type=MESH
        )
    lax.fori_loop(1, shards, greet, 0)
    for copy in (imp_in, asg_in, k_in, v_in, q_in):
        copy.start()

    imp_in.wait()
    part_weight = jnp.sum(imp_ref[...].astype(F32), axis=0, keepdims=True)
    kv_send[...] = jnp.broadcast_to(part_weight, (8, rows))
    for s in (0, 1, shards - 1):
        far_recv[s] = jnp.zeros((16, LANES), BF16)
    far_wide[...] = jnp.zeros_like(far_wide)

    pl.semaphore_wait(barrier, shards - 1 + kv_size - 1)
    kv_copies = [
        put(kv_send, kv_recv.at[s], kv_ss.at[s], kv_rs.at[s], (me, lax.rem(kv + s, kv_size)))
        for s in range(1, kv_size)
    ]

    asg_in.wait()
    asg = asg_ref[...]
    owner = jnp.right_shift(asg, rows.bit_length() - 1)
    target = jnp.bitwise_and(asg, rows - 1)
    distance = jnp.bitwise_and(owner - me, shards - 1)
    rank_row = lax.broadcasted_iota(jnp.int32, (16, rows), 0)
    distance_16 = jnp.broadcast_to(distance, (16, rows))
    wanted = jnp.where(rank_row == 0, 1, jnp.where(rank_row == 1, shards - 1, -1))
    marks = jnp.where(distance_16 == wanted, 1.0, 0.0).astype(BF16)
    earlier = jnp.where(
        lax.broadcasted_iota(jnp.int32, (rows, rows), 0)
        < lax.broadcasted_iota(jnp.int32, (rows, rows), 1),
        1.0, 0.0,
    ).astype(BF16)
    rank = dot(marks, earlier).astype(jnp.int32)
    key_next = jnp.where(distance == 1, rank[0:1], -1)
    key_prev = jnp.where(distance == shards - 1, rank[1:2], -1)
    far = jnp.where(distance >= 2, jnp.where(distance <= shards - 2, distance, -1), -1)

    def select(key, count):
        index = lax.broadcasted_iota(jnp.int32, (count, rows), 0)
        return jnp.where(jnp.broadcast_to(key, (count, rows)) == index, 1.0, 0.0)

    chosen = jnp.concatenate(
        [select(key_next, NEAR), select(key_prev, NEAR), select(far, shards)], axis=0
    )
    chosen_b = chosen.astype(BF16)
    k_in.wait()
    v_in.wait()
    out_rows = [dot(chosen_b, k_ref[...]), dot(chosen_b, v_ref[...])]
    meta_high = jnp.sum(
        chosen * jnp.right_shift(target, 7).astype(F32), axis=1, keepdims=True
    )
    meta_low = jnp.sum(
        chosen * jnp.bitwise_and(target, LANES - 1).astype(F32), axis=1, keepdims=True
    )
    for d in range(2):
        for part in range(2):
            near_send[d, :, part * width:(part + 1) * width] = out_rows[part][
                d * NEAR:(d + 1) * NEAR
            ].astype(BF16)
    for c in range(tiles):
        part, at = divmod(c, heads)
        far_wide[:, c, :] = out_rows[part][2 * NEAR:, at * LANES:(at + 1) * LANES]

    total_weight = part_weight
    for s, copy in enumerate(kv_copies, 1):
        copy.wait_recv()
        total_weight = total_weight + kv_recv[s, 0:1, :]
    weight = total_weight.astype(BF16).astype(F32)
    meta_weight = jnp.sum(chosen * weight, axis=1, keepdims=True)
    for m, meta in enumerate((meta_weight, meta_high, meta_low)):
        spread = jnp.broadcast_to(meta, (slots, LANES))
        for d in range(2):
            near_send[d, :, 2 * width + m * LANES:2 * width + (m + 1) * LANES] = spread[
                d * NEAR:(d + 1) * NEAR
            ].astype(BF16)
        far_wide[:, tiles + m, :] = spread[2 * NEAR:]
    far_send[...] = far_wide[...].astype(BF16)

    near_copies = [
        put(near_send.at[d], near_recv.at[d], near_ss.at[d], near_rs.at[d],
            (lax.rem(me + step, shards), kv))
        for d, step in enumerate((1, shards - 1))
    ]

    def far_copy(s):
        return pltpu.make_async_remote_copy(
            src_ref=far_send.at[s], dst_ref=far_recv.at[s],
            send_sem=far_ss.at[s], recv_sem=far_rs.at[s],
            device_id=(lax.rem(me + s, shards), kv), device_id_type=MESH,
        )

    def far_start(s, carry):
        far_copy(s).start()
        return carry

    def far_wait(s, carry):
        far_copy(s).wait()
        return carry

    lax.fori_loop(2, shards - 1, far_start, 0)

    home = jnp.where(distance == 0, target, -1)
    home_matrix = jnp.where(
        jnp.broadcast_to(home, (rows, rows))
        == lax.broadcasted_iota(jnp.int32, (rows, rows), 0),
        jnp.broadcast_to(weight, (rows, rows)), 0.0,
    ).astype(BF16)
    num[:, 0:width] = dot(home_matrix, k_ref[...])
    num[:, width:2 * width] = dot(home_matrix, v_ref[...])
    num[:, 2 * width:] = dot(home_matrix, jnp.ones((rows, LANES), BF16))
    q_in.wait()

    def turn_queries(j, carry):
        at = pl.ds(pl.multiple_of(j * 4 * LANES, 4 * LANES), 4 * LANES)
        group = q_ref[:, at]
        q_t[0:LANES, at] = jnp.concatenate(
            [group[:, n * LANES:(n + 1) * LANES].T for n in range(4)], axis=1
        )
        return carry

    lax.fori_loop(0, lanes // (4 * LANES), turn_queries, 0)
    q_t[LANES:, :] = jnp.ones((LANES, lanes), BF16)

    for copy in near_copies:
        copy.wait_recv()
    lax.fori_loop(2, shards - 1, far_wait, 0)

    far_wide[...] = far_recv[...].astype(F32)
    for d in range(2):
        arrived[d * NEAR:(d + 1) * NEAR, 0:2 * width] = near_recv[d, :, 0:2 * width]
    for c in range(tiles):
        arrived[2 * NEAR:, c * LANES:(c + 1) * LANES] = far_wide[:, c, :].astype(BF16)
    arrived[:, 2 * width:] = jnp.ones((slots, LANES), BF16)

    def meta_of(m):
        at = slice(2 * width + m * LANES, 2 * width + (m + 1) * LANES)
        return jnp.concatenate(
            [near_recv[0, :, at].astype(F32), near_recv[1, :, at].astype(F32),
             far_wide[:, tiles + m, :]], axis=0,
        )

    in_weight = meta_of(0)
    in_target = (meta_of(1) * LANES + meta_of(2)).astype(jnp.int32)
    lane = lax.broadcasted_iota(jnp.int32, (slots, LANES), 1)
    spread_t = jnp.concatenate(
        [jnp.where(in_target == lane + b * LANES, in_weight, 0.0) for b in range(rows // LANES)],
        axis=1,
    ).astype(BF16)

    num[...] += dot_t(spread_t, arrived[...])
    denominator = num[:, 2 * width:]
    kept = denominator > 0.0
    inverse = 1.0 / jnp.where(kept, denominator, 1.0)
    first_lane = lax.broadcasted_iota(jnp.int32, (rows, LANES), 1) == 0
    bias = jnp.where(first_lane, jnp.where(kept, 0.0, -1e30), 0.0).astype(BF16)
    for h in range(heads):
        at = slice(h * LANES, (h + 1) * LANES)
        far_at = slice(width + h * LANES, width + (h + 1) * LANES)
        key = num[:, at] * inverse
        key = jnp.where(kept, key, k_ref[:, at].astype(F32)).astype(BF16)
        mk_ref[:, at] = key
        k_ext[h, :, 0:LANES] = key
        k_ext[h, :, LANES:] = bias
        value = num[:, far_at] * inverse
        value = jnp.where(kept, value, v_ref[:, at].astype(F32)).astype(BF16)
        mv_ref[:, at] = value
        v_t[h, 0:LANES, :] = value.T
        v_t[h, LANES:, :] = jnp.ones((16, rows), BF16)

    def attend(columns):
        def score_of(column):
            queries = q_t[:, pl.ds(pl.multiple_of(column, LANES), piece)]
            return dot(k_ext[lax.div(column, group_lanes)], queries)

        results = []
        score = score_of(columns[0])
        for n, column in enumerate(columns):
            ahead = score_of(columns[n + 1]) if n + 1 < len(columns) else None
            peak = jnp.max(score, axis=0, keepdims=True)
            prob = jnp.exp2((score - peak) * coef).astype(BF16)
            both = dot(v_t[lax.div(column, group_lanes)], prob)
            results.append((both[0:LANES], peak, both[LANES:LANES + 1]))
            score = ahead
        return results

    def sub_of(u):
        return lax.rem(hi + u, high) if scatter else 0

    wide = rounds * piece

    def place(part, sub, r):
        return part * chunk + sub * wide + r * piece

    def line(s):
        return (lax.rem(hi + s, high) * PLANE + lo, kv)

    across = {p: (hi * PLANE + flip(lo, p), kv) for p in (1, 2, 3)}

    def hop(s, t):
        return [
            pltpu.make_async_remote_copy(
                src_ref=src.at[s, t], dst_ref=dst.at[s, t], send_sem=ss.at[s, t],
                recv_sem=rs.at[s, t], device_id=across[s], device_id_type=MESH,
            )
            for src, dst, ss, rs in (
                (s1_send, s1_recv, s1_ss, s1_rs), (l1_send, l1_recv, l1_ss, l1_rs),
            )
        ]

    def hop_line(t):
        return [
            pltpu.make_async_remote_copy(
                src_ref=src.at[t], dst_ref=dst.at[t], send_sem=ss.at[t],
                recv_sem=rs.at[t], device_id=line(t), device_id_type=MESH,
            )
            for src, dst, ss, rs in (
                (s2_send, s2_recv, s2_ss, s2_rs), (l2_send, l2_recv, l2_ss, l2_rs),
            )
        ]

    def work(t):
        steps = (3, 1, 2, 0)
        places = [place(flip(lo, s) if s else lo, sub_of(t), 0) for s in steps]
        for s, (o, m, l) in zip(steps, attend(places)):
            if s == 0:
                own_o[t] = o
                own_s[t] = stats(m, l)
            else:
                l1_send[s, t] = o.astype(BF16)
                s1_send[s, t] = stats(m, l)
        for s in (3, 1, 2):
            for copy in hop(s, t):
                copy.start()

    def gather_plane(t):
        parts = [(own_o[t], own_s[t, 0:1, :], own_s[t, 1:2, :])]
        for s in (1, 2, 3):
            for copy in hop(s, t):
                copy.wait_recv()
            parts.append(
                (l1_recv[s, t].astype(F32), s1_recv[s, t, 0:1, :], s1_recv[s, t, 1:2, :])
            )
        return combine(parts, coef)

    def forward(t):
        o, m, l = gather_plane(t)
        l2_send[t] = o.astype(BF16)
        s2_send[t] = stats(m, l)
        for copy in hop_line(t):
            copy.start()

    def turn(n, carry):
        work(lax.rem(n + 1, subs))

        @pl.when(n >= 2)
        def _():
            forward(n - 1)

        return carry

    def gather_line(r):
        o, m, l = gather_plane(0)
        base = r * high
        if scatter:
            parts = [(o, m, l)]
            for t in range(1, high):
                for copy in hop_line(t):
                    copy.wait_recv()
                parts.append((l2_recv[t].astype(F32), s2_recv[t, 0:1, :], s2_recv[t, 1:2, :]))
        else:
            l2_send[base] = o.astype(BF16)
            s2_send[base] = stats(m, l)
            l2_recv[base + hi] = o.astype(BF16)
            s2_recv[base + hi] = stats(m, l)
            for s in range(1, high):
                put(s2_send.at[base], s2_recv.at[base + hi], s2_ss.at[base + s],
                    s2_rs.at[base + hi], line(s))
                put(l2_send.at[base], l2_recv.at[base + hi], l2_ss.at[base + s],
                    l2_rs.at[base + hi], line(s))
            for s in range(1, high):
                other = base + lax.rem(hi + s, high)
                for src, dst, ss, rs in (
                    (s2_send, s2_recv, s2_ss, s2_rs), (l2_send, l2_recv, l2_ss, l2_rs),
                ):
                    pltpu.make_async_remote_copy(
                        src_ref=src.at[base], dst_ref=dst.at[other], send_sem=ss.at[base + s],
                        recv_sem=rs.at[other], device_id=line(s), device_id_type=MESH,
                    ).wait_recv()
            parts = [
                (l2_recv[base + j].astype(F32), s2_recv[base + j, 0:1, :],
                 s2_recv[base + j, 1:2, :])
                for j in range(high)
            ]
        return combine(parts, coef)

    def block(column):
        return out_ref.at[:, pl.ds(pl.multiple_of(column, LANES), piece)]

    def from_line(r, s, p=0):
        part = flip(lo, p) if p else lo
        return place(part, lax.rem(hi - s + high, high) if scatter else 0, r)

    def await_copy(view, ss, rs):
        pltpu.make_async_remote_copy(
            src_ref=view, dst_ref=view, send_sem=ss, recv_sem=rs,
            device_id=line(1), device_id_type=MESH,
        ).wait_recv()

    def straight(s):
        return s >= 2

    def to_plane(r, s):
        view, t = block(from_line(r, s)), r * subs + s
        for p in (3, 1, 2) if straight(s) else (1, 2):
            put(view, view, g1_ss.at[p, t], g1_rs.at[p, t], across[p])

    def finish(r):
        o, _, l = gather_line(r)
        result = o * (1.0 / l)
        mine = from_line(r, 0)
        for j in range(piece // LANES):
            at = pl.ds(pl.multiple_of(mine + j * LANES, LANES), LANES)
            out_ref[:, at] = result[:, j * LANES:(j + 1) * LANES].T.astype(BF16)
        if scatter:
            for s in range(1, high):
                t = r * high + s
                put(block(mine), block(mine), g2_ss.at[t], g2_rs.at[t], line(s))
        to_plane(r, 0)

    def spread_line(r, s):
        t = r * high + s
        await_copy(block(from_line(r, s)), g2_ss.at[t], g2_rs.at[t])
        to_plane(r, s)

    def pass_on(r, s):
        if straight(s):
            return
        p = 1 + (r + s) % 2
        t = r * subs + s
        view = block(from_line(r, s, p))
        await_copy(view, g1_ss.at[p, t], g1_rs.at[p, t])
        put(view, view, g1_ss.at[3, t], g1_rs.at[3, t], across[3 - p])

    def last_waits(r, s):
        t = r * subs + s
        for p in (1, 2, 3) if straight(s) else (2 - (r + s) % 2, 3):
            await_copy(block(from_line(r, s, p)), g1_ss.at[p, t], g1_rs.at[p, t])

    lax.fori_loop(0, subs, turn, 0)
    if scatter:
        forward(subs - 1)
    finish(rounds - 1)
    for s in range(subs):
        for r in range(rounds - 1):
            pass_on(r, s)
    for s in range(1, subs):
        spread_line(rounds - 1, s)
        pass_on(rounds - 1, s - 1)
    pass_on(rounds - 1, subs - 1)
    for r in range(rounds):
        for s in range(subs):
            last_waits(r, s)
    for copy in sent:
        copy.wait_send()

    def drain(t, carry):
        for s in (1, 2, 3):
            for copy in hop(s, t):
                copy.wait_send()
        if scatter:
            @pl.when(t >= 1)
            def _():
                for copy in hop_line(t):
                    copy.wait_send()
        return carry

    lax.fori_loop(0, subs, drain, 0)


def per_device(cache_keys, cache_values, importance, assignment, queries):
    shards = lax.axis_size("ctx")
    kv_size = lax.axis_size("kv")
    rows, width = cache_keys.shape
    lanes = queries.shape[1]
    high = shards // PLANE
    subs = high if (lanes // PLANE) % (high * LANES) == 0 else 1
    rounds = 1
    piece = lanes // PLANE // subs // rounds
    steps = rounds * subs
    heads = width // LANES
    slots = 2 * NEAR + shards
    wide = 2 * width + 3 * LANES
    dma = pltpu.SemaphoreType.DMA
    vmem = pl.BlockSpec(memory_space=pltpu.VMEM)
    hbm = pl.BlockSpec(memory_space=pltpu.HBM)
    body = functools.partial(kernel, shards, kv_size, subs, rounds, piece)
    shapes = (
        jax.ShapeDtypeStruct((rows, width), BF16),
        jax.ShapeDtypeStruct((rows, width), BF16),
        jax.ShapeDtypeStruct(queries.shape, BF16),
    )
    call = pl.pallas_call(
        body,
        out_shape=tuple(pltpu.VMEM(x.shape, x.dtype) for x in shapes),
        in_specs=[hbm] * 5,
        out_specs=(vmem,) * 3,
        scratch_shapes=[
            pltpu.VMEM((rows, width), BF16),
            pltpu.VMEM((rows, width), BF16),
            pltpu.VMEM(importance.shape, BF16),
            pltpu.VMEM((1, rows), jnp.int32),
            pltpu.VMEM(queries.shape, BF16),
            dma((5,)),
            pltpu.VMEM((8, rows), F32),
            pltpu.VMEM((kv_size, 8, rows), F32),
            pltpu.VMEM((2, NEAR, wide), BF16),
            pltpu.VMEM((2, NEAR, wide), BF16),
            pltpu.VMEM((shards, 16, LANES), BF16),
            pltpu.VMEM((shards, 16, LANES), BF16),
            pltpu.VMEM((shards, 16, LANES), F32),
            pltpu.VMEM((slots, 2 * width + LANES), BF16),
            pltpu.VMEM((rows, 2 * width + LANES), F32),
            pltpu.VMEM((2 * LANES, lanes), BF16),
            pltpu.VMEM((heads, rows, 2 * LANES), BF16),
            pltpu.VMEM((heads, LANES + 16, rows), BF16),
            pltpu.VMEM((PLANE, steps, LANES, piece), BF16),
            pltpu.VMEM((PLANE, steps, LANES, piece), BF16),
            pltpu.VMEM((PLANE, steps, 8, piece), F32),
            pltpu.VMEM((PLANE, steps, 8, piece), F32),
            pltpu.VMEM((steps, LANES, piece), F32),
            pltpu.VMEM((steps, 8, piece), F32),
            pltpu.VMEM((rounds * high, LANES, piece), BF16),
            pltpu.VMEM((rounds * high, LANES, piece), BF16),
            pltpu.VMEM((rounds * high, 8, piece), F32),
            pltpu.VMEM((rounds * high, 8, piece), F32),
            dma((kv_size,)), dma((kv_size,)),
            dma((2,)), dma((2,)),
            dma((shards,)), dma((shards,)),
            dma((PLANE, steps)), dma((PLANE, steps)),
            dma((PLANE, steps)), dma((PLANE, steps)),
            dma((rounds * high,)), dma((rounds * high,)),
            dma((rounds * high,)), dma((rounds * high,)),
            dma((rounds * high,)), dma((rounds * high,)),
            dma((PLANE, steps)), dma((PLANE, steps)),
        ],
        compiler_params=pltpu.CompilerParams(
            collective_id=0, has_side_effects=True, vmem_limit_bytes=40 * 1024 * 1024
        ),
    )
    operands = (cache_keys, cache_values, importance, assignment.reshape(1, rows), queries)
    return call(*(pltpu.with_memory_space_constraint(x, pltpu.HBM) for x in operands))


def solution(mesh):
    placed = (P("ctx", "kv"), P("ctx", "kv"), P("kv", "ctx"), P("ctx"), P(None, "kv"))
    return jax.shard_map(
        per_device,
        mesh=mesh,
        in_specs=placed,
        out_specs=(P("ctx", "kv"), P("ctx", "kv"), P(None, "kv")),
        check_vma=False,
    )
```

```python
import functools
import math

import jax
import jax.numpy as jnp
from jax import lax
from jax.experimental import pallas as pl
from jax.experimental.pallas import tpu as pltpu
from jax.sharding import PartitionSpec as P

NEAR = 16
LANES = 128
PLANE = 4
MESH = pl.DeviceIdType.MESH
F32 = jnp.float32
BF16 = jnp.bfloat16


def dot(a, b):
    return jnp.dot(a, b, preferred_element_type=F32)


def dot_t(a, b):
    return lax.dot_general(a, b, (((0,), (0,)), ((), ())), preferred_element_type=F32)


def flip(index, step):
    if step == 1:
        return index + 1 - 2 * lax.rem(index, 2)
    if step == 2:
        return index + 2 - 4 * lax.div(index, 2)
    return 3 - index


def combine(parts, coef):
    peak = functools.reduce(jnp.maximum, [m for _, m, _ in parts])
    total, weight = None, None
    for o, m, l in parts:
        factor = jnp.exp2((m - peak) * coef)
        o, l = o * factor, l * factor
        total = o if total is None else total + o
        weight = l if weight is None else weight + l
    return total, peak, weight


def stats(m, l):
    rows = lax.broadcasted_iota(jnp.int32, (8, m.shape[1]), 0)
    shape = (8, m.shape[1])
    return jnp.where(rows == 0, jnp.broadcast_to(m, shape), jnp.broadcast_to(l, shape))


def kernel(
    shards, kv_size, subs, rounds, piece,
    k_hbm, v_hbm, imp_hbm, asg_hbm, q_hbm,
    mk_ref, mv_ref, out_ref,
    k_ref, v_ref, imp_ref, asg_ref, q_ref, in_sems,
    kv_send, kv_recv, near_send, near_recv, far_send, far_recv, far_wide, arrived,
    num, q_t, k_ext, v_t,
    l1_send, l1_recv, s1_send, s1_recv, own_o, own_s,
    l2_send, l2_recv, s2_send, s2_recv,
    kv_ss, kv_rs, near_ss, near_rs, far_ss, far_rs,
    l1_ss, l1_rs, s1_ss, s1_rs, l2_ss, l2_rs, s2_ss, s2_rs,
    g2_ss, g2_rs, g1_ss, g1_rs,
):
    me = lax.axis_index("ctx")
    kv = lax.axis_index("kv")
    lo, hi = lax.rem(me, PLANE), lax.div(me, PLANE)
    high = shards // PLANE
    scatter = subs == high
    rows, width = k_ref.shape
    heads = width // LANES
    lanes = q_ref.shape[1]
    group_lanes = lanes // heads
    chunk = lanes // PLANE
    slots = 2 * NEAR + shards
    tiles = 2 * heads
    coef = math.log2(math.e) / math.sqrt(LANES)
    sent = []

    def put(src, dst, ss, rs, target):
        copy = pltpu.make_async_remote_copy(
            src_ref=src, dst_ref=dst, send_sem=ss, recv_sem=rs,
            device_id=target, device_id_type=MESH,
        )
        copy.start()
        sent.append(copy)
        return copy

    imp_in, asg_in, k_in, v_in, q_in = [
        pltpu.make_async_copy(src, dst, in_sems.at[n])
        for n, (src, dst) in enumerate((
            (imp_hbm, imp_ref), (asg_hbm, asg_ref), (k_hbm, k_ref), (v_hbm, v_ref),
            (q_hbm, q_ref),
        ))
    ]
    barrier = pltpu.get_barrier_semaphore()

    def greet(s, carry):
        pl.semaphore_signal(
            barrier, inc=1, device_id=(lax.rem(me + s, shards), kv), device_id_type=MESH
        )
        return carry

    for s in range(1, kv_size):
        pl.semaphore_signal(
            barrier, inc=1, device_id=(me, lax.rem(kv + s, kv_size)), device_id_type=MESH
        )
    lax.fori_loop(1, shards, greet, 0)
    for copy in (imp_in, asg_in, k_in, v_in, q_in):
        copy.start()

    imp_in.wait()
    part_weight = jnp.sum(imp_ref[...].astype(F32), axis=0, keepdims=True)
    kv_send[...] = jnp.broadcast_to(part_weight, (8, rows))
    for s in (0, 1, shards - 1):
        far_recv[s] = jnp.zeros((16, LANES), BF16)
    far_wide[...] = jnp.zeros_like(far_wide)

    pl.semaphore_wait(barrier, shards - 1 + kv_size - 1)
    kv_copies = [
        put(kv_send, kv_recv.at[s], kv_ss.at[s], kv_rs.at[s], (me, lax.rem(kv + s, kv_size)))
        for s in range(1, kv_size)
    ]

    asg_in.wait()
    asg = asg_ref[...]
    owner = jnp.right_shift(asg, rows.bit_length() - 1)
    target = jnp.bitwise_and(asg, rows - 1)
    distance = jnp.bitwise_and(owner - me, shards - 1)
    rank_row = lax.broadcasted_iota(jnp.int32, (16, rows), 0)
    distance_16 = jnp.broadcast_to(distance, (16, rows))
    wanted = jnp.where(rank_row == 0, 1, jnp.where(rank_row == 1, shards - 1, -1))
    marks = jnp.where(distance_16 == wanted, 1.0, 0.0).astype(BF16)
    earlier = jnp.where(
        lax.broadcasted_iota(jnp.int32, (rows, rows), 0)
        < lax.broadcasted_iota(jnp.int32, (rows, rows), 1),
        1.0, 0.0,
    ).astype(BF16)
    rank = dot(marks, earlier).astype(jnp.int32)
    key_next = jnp.where(distance == 1, rank[0:1], -1)
    key_prev = jnp.where(distance == shards - 1, rank[1:2], -1)
    far = jnp.where(distance >= 2, jnp.where(distance <= shards - 2, distance, -1), -1)

    def select(key, count):
        index = lax.broadcasted_iota(jnp.int32, (count, rows), 0)
        return jnp.where(jnp.broadcast_to(key, (count, rows)) == index, 1.0, 0.0)

    chosen = jnp.concatenate(
        [select(key_next, NEAR), select(key_prev, NEAR), select(far, shards)], axis=0
    )
    chosen_b = chosen.astype(BF16)
    k_in.wait()
    v_in.wait()
    out_rows = [dot(chosen_b, k_ref[...]), dot(chosen_b, v_ref[...])]
    meta_high = jnp.sum(
        chosen * jnp.right_shift(target, 7).astype(F32), axis=1, keepdims=True
    )
    meta_low = jnp.sum(
        chosen * jnp.bitwise_and(target, LANES - 1).astype(F32), axis=1, keepdims=True
    )
    for d in range(2):
        for part in range(2):
            near_send[d, :, part * width:(part + 1) * width] = out_rows[part][
                d * NEAR:(d + 1) * NEAR
            ].astype(BF16)
    for c in range(tiles):
        part, at = divmod(c, heads)
        far_wide[:, c, :] = out_rows[part][2 * NEAR:, at * LANES:(at + 1) * LANES]

    total_weight = part_weight
    for s, copy in enumerate(kv_copies, 1):
        copy.wait_recv()
        total_weight = total_weight + kv_recv[s, 0:1, :]
    weight = total_weight.astype(BF16).astype(F32)
    meta_weight = jnp.sum(chosen * weight, axis=1, keepdims=True)
    for m, meta in enumerate((meta_weight, meta_high, meta_low)):
        spread = jnp.broadcast_to(meta, (slots, LANES))
        for d in range(2):
            near_send[d, :, 2 * width + m * LANES:2 * width + (m + 1) * LANES] = spread[
                d * NEAR:(d + 1) * NEAR
            ].astype(BF16)
        far_wide[:, tiles + m, :] = spread[2 * NEAR:]
    far_send[...] = far_wide[...].astype(BF16)

    near_copies = [
        put(near_send.at[d], near_recv.at[d], near_ss.at[d], near_rs.at[d],
            (lax.rem(me + step, shards), kv))
        for d, step in enumerate((1, shards - 1))
    ]

    def far_copy(s):
        return pltpu.make_async_remote_copy(
            src_ref=far_send.at[s], dst_ref=far_recv.at[s],
            send_sem=far_ss.at[s], recv_sem=far_rs.at[s],
            device_id=(lax.rem(me + s, shards), kv), device_id_type=MESH,
        )

    def far_start(s, carry):
        far_copy(s).start()
        return carry

    def far_wait(s, carry):
        far_copy(s).wait()
        return carry

    lax.fori_loop(2, shards - 1, far_start, 0)

    home = jnp.where(distance == 0, target, -1)
    home_matrix = jnp.where(
        jnp.broadcast_to(home, (rows, rows))
        == lax.broadcasted_iota(jnp.int32, (rows, rows), 0),
        jnp.broadcast_to(weight, (rows, rows)), 0.0,
    ).astype(BF16)
    num[:, 0:width] = dot(home_matrix, k_ref[...])
    num[:, width:2 * width] = dot(home_matrix, v_ref[...])
    num[:, 2 * width:] = dot(home_matrix, jnp.ones((rows, LANES), BF16))
    q_in.wait()

    def turn_queries(j, carry):
        at = pl.ds(pl.multiple_of(j * 4 * LANES, 4 * LANES), 4 * LANES)
        group = q_ref[:, at]
        q_t[0:LANES, at] = jnp.concatenate(
            [group[:, n * LANES:(n + 1) * LANES].T for n in range(4)], axis=1
        )
        return carry

    lax.fori_loop(0, lanes // (4 * LANES), turn_queries, 0)
    q_t[LANES:, :] = jnp.ones((LANES, lanes), BF16)

    for copy in near_copies:
        copy.wait_recv()
    lax.fori_loop(2, shards - 1, far_wait, 0)

    far_wide[...] = far_recv[...].astype(F32)
    for d in range(2):
        arrived[d * NEAR:(d + 1) * NEAR, 0:2 * width] = near_recv[d, :, 0:2 * width]
    for c in range(tiles):
        arrived[2 * NEAR:, c * LANES:(c + 1) * LANES] = far_wide[:, c, :].astype(BF16)
    arrived[:, 2 * width:] = jnp.ones((slots, LANES), BF16)

    def meta_of(m):
        at = slice(2 * width + m * LANES, 2 * width + (m + 1) * LANES)
        return jnp.concatenate(
            [near_recv[0, :, at].astype(F32), near_recv[1, :, at].astype(F32),
             far_wide[:, tiles + m, :]], axis=0,
        )

    in_weight = meta_of(0)
    in_target = (meta_of(1) * LANES + meta_of(2)).astype(jnp.int32)
    lane = lax.broadcasted_iota(jnp.int32, (slots, LANES), 1)
    spread_t = jnp.concatenate(
        [jnp.where(in_target == lane + b * LANES, in_weight, 0.0) for b in range(rows // LANES)],
        axis=1,
    ).astype(BF16)

    num[...] += dot_t(spread_t, arrived[...])
    denominator = num[:, 2 * width:]
    kept = denominator > 0.0
    inverse = 1.0 / jnp.where(kept, denominator, 1.0)
    first_lane = lax.broadcasted_iota(jnp.int32, (rows, LANES), 1) == 0
    bias = jnp.where(first_lane, jnp.where(kept, 0.0, -1e30), 0.0).astype(BF16)
    for h in range(heads):
        at = slice(h * LANES, (h + 1) * LANES)
        far_at = slice(width + h * LANES, width + (h + 1) * LANES)
        key = num[:, at] * inverse
        key = jnp.where(kept, key, k_ref[:, at].astype(F32)).astype(BF16)
        mk_ref[:, at] = key
        k_ext[h, :, 0:LANES] = key
        k_ext[h, :, LANES:] = bias
        value = num[:, far_at] * inverse
        value = jnp.where(kept, value, v_ref[:, at].astype(F32)).astype(BF16)
        mv_ref[:, at] = value
        v_t[h, 0:LANES, :] = value.T
        v_t[h, LANES:, :] = jnp.ones((16, rows), BF16)

    def attend(columns):
        def score_of(column):
            queries = q_t[:, pl.ds(pl.multiple_of(column, LANES), piece)]
            return dot(k_ext[lax.div(column, group_lanes)], queries)

        score = score_of(columns[0])
        for n, column in enumerate(columns):
            ahead = score_of(columns[n + 1]) if n + 1 < len(columns) else None
            peak = jnp.max(score, axis=0, keepdims=True)
            prob = jnp.exp2((score - peak) * coef).astype(BF16)
            both = dot(v_t[lax.div(column, group_lanes)], prob)
            yield both[0:LANES], peak, both[LANES:LANES + 1]
            score = ahead

    def sub_of(u):
        return lax.rem(hi + u, high) if scatter else 0

    wide = rounds * piece

    def place(part, sub, r):
        return part * chunk + sub * wide + r * piece

    def line(s):
        return (lax.rem(hi + s, high) * PLANE + lo, kv)

    across = {p: (hi * PLANE + flip(lo, p), kv) for p in (1, 2, 3)}

    def hop(s, t):
        return [
            pltpu.make_async_remote_copy(
                src_ref=src.at[s, t], dst_ref=dst.at[s, t], send_sem=ss.at[s, t],
                recv_sem=rs.at[s, t], device_id=across[s], device_id_type=MESH,
            )
            for src, dst, ss, rs in (
                (s1_send, s1_recv, s1_ss, s1_rs), (l1_send, l1_recv, l1_ss, l1_rs),
            )
        ]

    def hop_line(t):
        return [
            pltpu.make_async_remote_copy(
                src_ref=src.at[t], dst_ref=dst.at[t], send_sem=ss.at[t],
                recv_sem=rs.at[t], device_id=line(t), device_id_type=MESH,
            )
            for src, dst, ss, rs in (
                (s2_send, s2_recv, s2_ss, s2_rs), (l2_send, l2_recv, l2_ss, l2_rs),
            )
        ]

    def work(t):
        steps = (3, 1, 2, 0)
        places = [place(flip(lo, s) if s else lo, sub_of(t), 0) for s in steps]
        for s, (o, m, l) in zip(steps, attend(places)):
            if s == 0:
                own_o[t] = o
                own_s[t] = stats(m, l)
            else:
                l1_send[s, t] = o.astype(BF16)
                s1_send[s, t] = stats(m, l)
                for copy in hop(s, t):
                    copy.start()

    def gather_plane(t):
        parts = [(own_o[t], own_s[t, 0:1, :], own_s[t, 1:2, :])]
        for s in (1, 2, 3):
            for copy in hop(s, t):
                copy.wait_recv()
            parts.append(
                (l1_recv[s, t].astype(F32), s1_recv[s, t, 0:1, :], s1_recv[s, t, 1:2, :])
            )
        return combine(parts, coef)

    def forward(t):
        o, m, l = gather_plane(t)
        l2_send[t] = o.astype(BF16)
        s2_send[t] = stats(m, l)
        for copy in hop_line(t):
            copy.start()

    def turn(n, carry):
        work(lax.rem(n + 1, subs))

        @pl.when(n >= 2)
        def _():
            forward(n - 1)

        return carry

    def gather_line(r):
        o, m, l = gather_plane(0)
        base = r * high
        if scatter:
            parts = [(o, m, l)]
            for t in range(1, high):
                for copy in hop_line(t):
                    copy.wait_recv()
                parts.append((l2_recv[t].astype(F32), s2_recv[t, 0:1, :], s2_recv[t, 1:2, :]))
        else:
            l2_send[base] = o.astype(BF16)
            s2_send[base] = stats(m, l)
            l2_recv[base + hi] = o.astype(BF16)
            s2_recv[base + hi] = stats(m, l)
            for s in range(1, high):
                put(s2_send.at[base], s2_recv.at[base + hi], s2_ss.at[base + s],
                    s2_rs.at[base + hi], line(s))
                put(l2_send.at[base], l2_recv.at[base + hi], l2_ss.at[base + s],
                    l2_rs.at[base + hi], line(s))
            for s in range(1, high):
                other = base + lax.rem(hi + s, high)
                for src, dst, ss, rs in (
                    (s2_send, s2_recv, s2_ss, s2_rs), (l2_send, l2_recv, l2_ss, l2_rs),
                ):
                    pltpu.make_async_remote_copy(
                        src_ref=src.at[base], dst_ref=dst.at[other], send_sem=ss.at[base + s],
                        recv_sem=rs.at[other], device_id=line(s), device_id_type=MESH,
                    ).wait_recv()
            parts = [
                (l2_recv[base + j].astype(F32), s2_recv[base + j, 0:1, :],
                 s2_recv[base + j, 1:2, :])
                for j in range(high)
            ]
        return combine(parts, coef)

    def block(column):
        return out_ref.at[:, pl.ds(pl.multiple_of(column, LANES), piece)]

    def from_line(r, s, p=0):
        part = flip(lo, p) if p else lo
        return place(part, lax.rem(hi - s + high, high) if scatter else 0, r)

    def await_copy(view, ss, rs):
        pltpu.make_async_remote_copy(
            src_ref=view, dst_ref=view, send_sem=ss, recv_sem=rs,
            device_id=line(1), device_id_type=MESH,
        ).wait_recv()

    def straight(s):
        return s >= 2

    def to_plane(r, s):
        view, t = block(from_line(r, s)), r * subs + s
        for p in (3, 1, 2) if straight(s) else (1, 2):
            put(view, view, g1_ss.at[p, t], g1_rs.at[p, t], across[p])

    def finish(r):
        o, _, l = gather_line(r)
        result = o * (1.0 / l)
        mine = from_line(r, 0)
        for j in range(piece // LANES):
            at = pl.ds(pl.multiple_of(mine + j * LANES, LANES), LANES)
            out_ref[:, at] = result[:, j * LANES:(j + 1) * LANES].T.astype(BF16)
        if scatter:
            for s in range(1, high):
                t = r * high + s
                put(block(mine), block(mine), g2_ss.at[t], g2_rs.at[t], line(s))
        to_plane(r, 0)

    def spread_line(r, s):
        t = r * high + s
        await_copy(block(from_line(r, s)), g2_ss.at[t], g2_rs.at[t])
        to_plane(r, s)

    def pass_on(r, s):
        if straight(s):
            return
        p = 1 + (r + s) % 2
        t = r * subs + s
        view = block(from_line(r, s, p))
        await_copy(view, g1_ss.at[p, t], g1_rs.at[p, t])
        put(view, view, g1_ss.at[3, t], g1_rs.at[3, t], across[3 - p])

    def last_waits(r, s):
        t = r * subs + s
        for p in (1, 2, 3) if straight(s) else (2 - (r + s) % 2, 3):
            await_copy(block(from_line(r, s, p)), g1_ss.at[p, t], g1_rs.at[p, t])

    lax.fori_loop(0, subs, turn, 0)
    if scatter:
        forward(subs - 1)
    finish(rounds - 1)
    for s in range(subs):
        for r in range(rounds - 1):
            pass_on(r, s)
    for s in range(1, subs):
        spread_line(rounds - 1, s)
        pass_on(rounds - 1, s - 1)
    pass_on(rounds - 1, subs - 1)
    for r in range(rounds):
        for s in range(subs):
            last_waits(r, s)
    for copy in sent:
        copy.wait_send()

    def drain(t, carry):
        for s in (1, 2, 3):
            for copy in hop(s, t):
                copy.wait_send()
        if scatter:
            @pl.when(t >= 1)
            def _():
                for copy in hop_line(t):
                    copy.wait_send()
        return carry

    lax.fori_loop(0, subs, drain, 0)


def per_device(cache_keys, cache_values, importance, assignment, queries):
    shards = lax.axis_size("ctx")
    kv_size = lax.axis_size("kv")
    rows, width = cache_keys.shape
    lanes = queries.shape[1]
    high = shards // PLANE
    subs = high if (lanes // PLANE) % (high * LANES) == 0 else 1
    rounds = 1
    piece = lanes // PLANE // subs // rounds
    steps = rounds * subs
    heads = width // LANES
    slots = 2 * NEAR + shards
    wide = 2 * width + 3 * LANES
    dma = pltpu.SemaphoreType.DMA
    vmem = pl.BlockSpec(memory_space=pltpu.VMEM)
    hbm = pl.BlockSpec(memory_space=pltpu.HBM)
    body = functools.partial(kernel, shards, kv_size, subs, rounds, piece)
    shapes = (
        jax.ShapeDtypeStruct((rows, width), BF16),
        jax.ShapeDtypeStruct((rows, width), BF16),
        jax.ShapeDtypeStruct(queries.shape, BF16),
    )
    call = pl.pallas_call(
        body,
        out_shape=tuple(pltpu.VMEM(x.shape, x.dtype) for x in shapes),
        in_specs=[hbm] * 5,
        out_specs=(vmem,) * 3,
        scratch_shapes=[
            pltpu.VMEM((rows, width), BF16),
            pltpu.VMEM((rows, width), BF16),
            pltpu.VMEM(importance.shape, BF16),
            pltpu.VMEM((1, rows), jnp.int32),
            pltpu.VMEM(queries.shape, BF16),
            dma((5,)),
            pltpu.VMEM((8, rows), F32),
            pltpu.VMEM((kv_size, 8, rows), F32),
            pltpu.VMEM((2, NEAR, wide), BF16),
            pltpu.VMEM((2, NEAR, wide), BF16),
            pltpu.VMEM((shards, 16, LANES), BF16),
            pltpu.VMEM((shards, 16, LANES), BF16),
            pltpu.VMEM((shards, 16, LANES), F32),
            pltpu.VMEM((slots, 2 * width + LANES), BF16),
            pltpu.VMEM((rows, 2 * width + LANES), F32),
            pltpu.VMEM((2 * LANES, lanes), BF16),
            pltpu.VMEM((heads, rows, 2 * LANES), BF16),
            pltpu.VMEM((heads, LANES + 16, rows), BF16),
            pltpu.VMEM((PLANE, steps, LANES, piece), BF16),
            pltpu.VMEM((PLANE, steps, LANES, piece), BF16),
            pltpu.VMEM((PLANE, steps, 8, piece), F32),
            pltpu.VMEM((PLANE, steps, 8, piece), F32),
            pltpu.VMEM((steps, LANES, piece), F32),
            pltpu.VMEM((steps, 8, piece), F32),
            pltpu.VMEM((rounds * high, LANES, piece), BF16),
            pltpu.VMEM((rounds * high, LANES, piece), BF16),
            pltpu.VMEM((rounds * high, 8, piece), F32),
            pltpu.VMEM((rounds * high, 8, piece), F32),
            dma((kv_size,)), dma((kv_size,)),
            dma((2,)), dma((2,)),
            dma((shards,)), dma((shards,)),
            dma((PLANE, steps)), dma((PLANE, steps)),
            dma((PLANE, steps)), dma((PLANE, steps)),
            dma((rounds * high,)), dma((rounds * high,)),
            dma((rounds * high,)), dma((rounds * high,)),
            dma((rounds * high,)), dma((rounds * high,)),
            dma((PLANE, steps)), dma((PLANE, steps)),
        ],
        compiler_params=pltpu.CompilerParams(
            collective_id=0, has_side_effects=True, vmem_limit_bytes=40 * 1024 * 1024
        ),
    )
    operands = (cache_keys, cache_values, importance, assignment.reshape(1, rows), queries)
    return call(*(pltpu.with_memory_space_constraint(x, pltpu.HBM) for x in operands))


def solution(mesh):
    placed = (P("ctx", "kv"), P("ctx", "kv"), P("kv", "ctx"), P("ctx"), P(None, "kv"))
    return jax.shard_map(
        per_device,
        mesh=mesh,
        in_specs=placed,
        out_specs=(P("ctx", "kv"), P("ctx", "kv"), P(None, "kv")),
        check_vma=False,
    )
```
